256 devices in a mesh: stretch: 32 (over z, x_hi, core), head: 8 (over x_lo, y).
Axes of the slice: x: 4 (x_hi: 2, x_lo: 2; x = x_hi * 2 + x_lo), y: 4, z: 8, core: 2. Of those that a mesh axis runs over, the one named last changes fastest.
Arguments:
- queries: bfloat16 [32768, 3072], P(('stretch', 'head')), as said below
- keys: bfloat16 [32768, 3072], P(('stretch', 'head')), as said below
- values: bfloat16 [32768, 3072], P(('stretch', 'head')), may hold values from -6 to 6
- visible: int32 [32], replicated, may hold values from 0 to 4, as said below
- lengths: int32 [32], replicated, may hold values from 512 to 1024, as said below
Outputs:
- attended: bfloat16 [32768, 3072], P(('stretch', 'head'))
The draws below stay inside these ranges and needn't reach their ends.
Inputs may be any that keep to these rules, and one draw needn't show every extreme that they name: `queries`: every entry lies in -5 to 5. `keys`: every entry lies in -5 to 5. Some stretch at index 4 or later has visible = 4. `lengths`: some stretch is full.
All inputs are finite; a program needn't handle non-finite values.
Results may differ from the reference program's by a relative error of at most 0.0047.
Values may be sent and summed in bfloat16 or wider, within the bound.
No kernel may reach another device: no remote copies, remote signals or barrier semaphores. Data moves between devices by JAX's collectives and lax.ppermute only.
A program may use at most 128 MiB of HBM per device.

```python
import jax
import jax.numpy as jnp
from jax import lax

HEADS = 24
HEAD_DIM = 128
SPAN = 4
STRETCH_TOK = 1024
STRETCHES = 32
TOKENS = 32768


def draw_keys(key, part):
    key = jax.random.fold_in(key, 11)
    width = HEADS * HEAD_DIM
    base = jnp.clip(jax.random.normal(key, (TOKENS, width), jnp.float32), -5.0, 5.0)
    return base.astype(jnp.bfloat16)


def draw_queries(key, part):
    key = jax.random.fold_in(key, 23)
    width = HEADS * HEAD_DIM
    base = jnp.clip(jax.random.normal(key, (TOKENS, width), jnp.float32), -5.0, 5.0)
    return base.astype(jnp.bfloat16)


def draw_visible(key, part):
    key = jax.random.fold_in(key, 37)
    first, second = jax.random.split(key)
    counts = jax.random.randint(first, (STRETCHES,), 0, SPAN + 1)
    where_most = jax.random.randint(second, (), SPAN, STRETCHES)
    return counts.at[where_most].set(SPAN).astype(jnp.int32)


def draw_lengths(key, part):
    key = jax.random.fold_in(key, 53)
    first, second = jax.random.split(key)
    sizes = jax.random.randint(first, (STRETCHES,), STRETCH_TOK // 2, STRETCH_TOK + 1)
    where_full = jax.random.randint(second, (), 0, STRETCHES)
    return sizes.at[where_full].set(STRETCH_TOK).astype(jnp.int32)


def shard_levels(own_key, extent, cuts, least, high):
    def one(dim, blocks):
        steps = jax.random.uniform(jax.random.fold_in(jax.random.fold_in(own_key, 6), dim), (blocks,), jnp.float32, least / len(cuts), high / len(cuts))
        return jnp.repeat(jnp.exp(steps), extent[dim] // blocks).reshape((-1,) + (1,) * (len(extent) - dim - 1))

    gain = one(*cuts[0])
    for cut in cuts[1:]:
        gain = gain * one(*cut)
    return gain


def centred(own_key, extent, deviation, reach, cuts=(), held_as=jnp.bfloat16):
    factor_of = shard_levels(own_key, extent, cuts, -0.22, 0.18) if cuts else 1.0
    drawn = jax.random.normal(own_key, extent, jnp.float32) * deviation * factor_of
    return jnp.minimum(jnp.maximum(drawn, -reach), reach).astype(held_as)


def setup_inputs(seed: int = 0) -> dict:
    seeds = jax.random.split(jax.random.key(seed), 6)
    return {
        "queries": draw_queries(jax.random.fold_in(seeds[5], 71), 0),
        "keys": draw_keys(jax.random.fold_in(seeds[5], 71), 0),
        "values": centred(seeds[2], (TOKENS, HEADS * HEAD_DIM), 1.0, 6.0, ((0, 256),)),
        "visible": draw_visible(jax.random.fold_in(seeds[5], 71), 0),
        "lengths": draw_lengths(jax.random.fold_in(seeds[5], 71), 0),
    }


def reference(queries, keys, values, visible, lengths):
    width = HEADS * HEAD_DIM
    q4 = queries.reshape(STRETCHES, STRETCH_TOK, HEADS, HEAD_DIM)
    k4 = keys.reshape(STRETCHES, STRETCH_TOK, HEADS, HEAD_DIM)
    v4 = values.reshape(STRETCHES, STRETCH_TOK, HEADS, HEAD_DIM)
    places = jnp.arange(STRETCH_TOK, dtype=jnp.int32)

    def one_stretch(stretch_id):
        query_block = lax.dynamic_index_in_dim(q4, stretch_id, 0, keepdims=False)
        key_parts, value_parts, usable_parts = [], [], []
        for back in range(SPAN + 1):
            source = jnp.maximum(stretch_id - back, 0).astype(jnp.int32)
            key_parts.append(lax.dynamic_index_in_dim(k4, source, 0, keepdims=False))
            value_parts.append(lax.dynamic_index_in_dim(v4, source, 0, keepdims=False))
            if back == 0:
                seen = jnp.array(True)
            else:
                seen = back <= jnp.minimum(visible[stretch_id], stretch_id)
            usable_parts.append(jnp.logical_and(seen, places < lengths[source]))
        key_all = jnp.concatenate(key_parts, 0).astype(jnp.float32)
        value_all = jnp.concatenate(value_parts, 0).astype(jnp.float32)
        usable = jnp.concatenate(usable_parts, 0)
        scores = jnp.einsum("qhd,khd->hqk", query_block.astype(jnp.float32), key_all) * (HEAD_DIM ** -0.5)
        scores = jnp.where(usable[None, None, :], scores, -jnp.inf)
        largest = jnp.max(scores, axis=2, keepdims=True)
        weights = jnp.exp(scores - largest)
        total = jnp.sum(weights, axis=2)
        rounded = weights.astype(jnp.bfloat16).astype(jnp.float32)
        mixed = jnp.einsum("hqk,khd->qhd", rounded, value_all)
        mixed = mixed / jnp.transpose(total)[:, :, None]
        mixed = jnp.where((places < lengths[stretch_id])[:, None, None], mixed, 0.0)
        return mixed.reshape(STRETCH_TOK, width).astype(jnp.bfloat16)

    result = lax.map(one_stretch, jnp.arange(STRETCHES, dtype=jnp.int32))
    return result.reshape(TOKENS, width)
```

```python
import functools
import math

import jax
import jax.numpy as jnp
from jax import lax
from jax.experimental import pallas as pl
from jax.experimental.pallas import tpu as pltpu
from jax.sharding import Mesh
from jax.sharding import PartitionSpec as P

HEAD_DIM = 128
ROWS = 128
GROUPS = 8
HALF = ROWS // 2
PLANE = 4
TILE = 512
TILES = 6
Q_ROWS = ROWS + HALF
KV_ROWS = 2 * ROWS
PAYLOAD = Q_ROWS + 2 * KV_ROWS
SCALE = HEAD_DIM**-0.5 * math.log2(math.e)
LOWEST = -1e30
AXES = ("z", "xh", "core", "head")
BIG = pltpu.CompilerParams(vmem_limit_bytes=48 * 2**20)


def pack_all(q_ref, k_ref, v_ref, out_ref):
    middle = slice(HEAD_DIM, 2 * HEAD_DIM)
    for half in range(2):
        own = slice(2 * HEAD_DIM * half, 2 * HEAD_DIM * half + HEAD_DIM)
        out_ref[half, 0, 0:ROWS] = q_ref[:, own]
        out_ref[half, 0, ROWS:Q_ROWS] = q_ref[half * HALF : (half + 1) * HALF, middle]
        at = Q_ROWS
        for ref in (k_ref, v_ref):
            out_ref[half, 0, at : at + ROWS] = ref[:, own]
            out_ref[half, 0, at + ROWS : at + KV_ROWS] = ref[:, middle]
            at += KV_ROWS


def pack_one(v_ref, out_ref):
    for half in range(2):
        own = slice(2 * HEAD_DIM * half, 2 * HEAD_DIM * half + HEAD_DIM)
        out_ref[half, 0, 0:ROWS] = v_ref[:, own]
        out_ref[half, 0, ROWS:KV_ROWS] = v_ref[:, HEAD_DIM : 2 * HEAD_DIM]


def pack(body, rows, *arrays):
    return pl.pallas_call(
        body,
        grid=(GROUPS,),
        in_specs=[pl.BlockSpec((ROWS, 3 * HEAD_DIM), lambda g: (0, g))] * len(arrays),
        out_specs=pl.BlockSpec((2, 1, rows, HEAD_DIM), lambda g: (0, g, 0, 0)),
        out_shape=jax.ShapeDtypeStruct((2, GROUPS, rows, HEAD_DIM), jnp.bfloat16),
    )(*arrays)


def unpack_body(in_ref, out_ref):
    out_ref[:, 0:HEAD_DIM] = in_ref[0, 0, 0:ROWS]
    out_ref[0:HALF, HEAD_DIM : 2 * HEAD_DIM] = in_ref[0, 0, ROWS:Q_ROWS]
    out_ref[HALF:ROWS, HEAD_DIM : 2 * HEAD_DIM] = in_ref[1, 0, ROWS:Q_ROWS]
    out_ref[:, 2 * HEAD_DIM : 3 * HEAD_DIM] = in_ref[1, 0, 0:ROWS]


def unpack(array):
    return pl.pallas_call(
        unpack_body,
        grid=(GROUPS,),
        in_specs=[pl.BlockSpec((2, 1, Q_ROWS, HEAD_DIM), lambda g: (0, g, 0, 0))],
        out_specs=pl.BlockSpec((ROWS, 3 * HEAD_DIM), lambda g: (0, g)),
        out_shape=jax.ShapeDtypeStruct((ROWS, GROUPS * 3 * HEAD_DIM), jnp.bfloat16),
    )(array)


def stage_queries(q_ref, q_scr):
    for slot in range(2):
        for i in range(2):
            q_scr[3 * slot + i] = q_ref[slot, 4 * i : 4 * i + 4, 0:ROWS].reshape(TILE, HEAD_DIM)
        q_scr[3 * slot + 2] = q_ref[slot, :, ROWS:Q_ROWS].reshape(TILE, HEAD_DIM)


def fold(t, q_scr, acc_ref, top_ref, keys, values, limit):
    q = q_scr[t]
    scores = lax.dot_general(
        q, keys, (((1,), (1,)), ((), ())), preferred_element_type=jnp.float32
    ) * SCALE
    if limit is not None:
        column = lax.broadcasted_iota(jnp.int32, scores.shape, 1)
        scores = jnp.where(column < limit, scores, LOWEST)
    old = top_ref[t]
    new = jnp.maximum(old, jnp.max(scores, axis=1, keepdims=True))
    weights = jnp.exp2(scores - jnp.concatenate([new] * (TILE // HEAD_DIM), 1))
    decay = jnp.exp2(old - new)
    wide = jnp.concatenate([values, jnp.ones_like(values)], 1)
    mixed = jnp.dot(weights.astype(jnp.bfloat16), wide, preferred_element_type=jnp.float32)
    acc_ref[t] = acc_ref[t] * jnp.concatenate([decay, decay], 1) + mixed
    top_ref[t] = new


def sweep(earlier, visible_ref, lengths_ref, q_scr, acc_ref, top_ref, sources):
    z, core = lax.axis_index("z"), lax.axis_index("core")

    def tile(t, carry):
        slot = t // 3
        shared = (t % 3) // 2
        stretch = PLANE * z + 2 * slot + core
        reach = jnp.minimum(visible_ref[stretch], stretch)

        def column(x, carry):
            for other, (k_ref, k_at, v_ref, v_at) in enumerate(sources):
                back = earlier * PLANE + 2 * (slot - x) + other * (2 * core - 1)
                seen = jnp.logical_and(back >= 0, back <= reach)
                length = lengths_ref[jnp.maximum(stretch - back, 0)]
                k_from = pl.multiple_of(k_at + ROWS * shared, HALF)
                v_from = pl.multiple_of(v_at + ROWS * shared, HALF)
                for part in range(2):

                    @pl.when(jnp.logical_and(seen, length > part * TILE))
                    def _():
                        blocks = slice(4 * part, 4 * part + 4)
                        keys = k_ref[x, blocks, pl.ds(k_from, ROWS)].reshape(TILE, HEAD_DIM)
                        values = v_ref[x, blocks, pl.ds(v_from, ROWS)].reshape(TILE, HEAD_DIM)
                        limit = None if part == 0 else length - TILE
                        fold(t, q_scr, acc_ref, top_ref, keys, values, limit)

            return carry

        return lax.fori_loop(0, 2, column, carry)

    lax.fori_loop(0, TILES, tile, 0)


def own_body(visible_ref, lengths_ref, here_ref, mate_ref, acc_ref, top_ref, q_scr):
    stage_queries(here_ref, q_scr)
    acc_ref[...] = jnp.zeros_like(acc_ref)
    top_ref[...] = jnp.full_like(top_ref, LOWEST)
    sources = [(ref, Q_ROWS, ref, Q_ROWS + KV_ROWS) for ref in (here_ref, mate_ref)]
    sweep(0, visible_ref, lengths_ref, q_scr, acc_ref, top_ref, sources)


def earlier_body(
    visible_ref, lengths_ref, q_ref, k_here, k_mate, v_here, v_mate, acc_in, top_in,
    out_ref, acc_ref, top_ref, q_scr,
):
    stage_queries(q_ref, q_scr)
    acc_ref[...] = acc_in[...]
    top_ref[...] = top_in[...]
    sources = [(k_here, 0, v_here, 0), (k_mate, 0, v_mate, 0)]
    sweep(1, visible_ref, lengths_ref, q_scr, acc_ref, top_ref, sources)
    z, xh, core = (lax.axis_index(name) for name in ("z", "xh", "core"))
    row = lax.broadcasted_iota(jnp.int32, (TILE, HEAD_DIM), 0)
    for slot in range(2):
        length = lengths_ref[PLANE * z + 2 * slot + core]
        for i in range(3):
            t = 3 * slot + i
            if i < 2:
                token = TILE * i + row
            else:
                token = (row // HALF) * ROWS + xh * HALF + row % HALF
            mixed = acc_ref[t, :, 0:HEAD_DIM] / acc_ref[t, :, HEAD_DIM:]
            mixed = jnp.where(token < length, mixed, 0.0).astype(jnp.bfloat16)
            if i < 2:
                out_ref[slot, 4 * i : 4 * i + 4, 0:ROWS] = mixed.reshape(4, ROWS, HEAD_DIM)
            else:
                out_ref[slot, :, ROWS:Q_ROWS] = mixed.reshape(GROUPS, HALF, HEAD_DIM)


SMEM = pl.BlockSpec(memory_space=pltpu.SMEM)
WHOLE = pl.BlockSpec(memory_space=pltpu.VMEM)
STATE = [
    jax.ShapeDtypeStruct((TILES, TILE, 2 * HEAD_DIM), jnp.float32),
    jax.ShapeDtypeStruct((TILES, TILE, HEAD_DIM), jnp.float32),
]
QUERY_SCRATCH = pltpu.VMEM((TILES, TILE, HEAD_DIM), jnp.bfloat16)


def attend_own(visible, lengths, here, mate):
    return pl.pallas_call(
        own_body,
        in_specs=[SMEM, SMEM, WHOLE, WHOLE],
        out_specs=[WHOLE, WHOLE],
        out_shape=STATE,
        scratch_shapes=[QUERY_SCRATCH],
        compiler_params=BIG,
        cost_estimate=pl.CostEstimate(flops=5 * 10**9, bytes_accessed=10**7, transcendentals=10**7),
    )(visible, lengths, here, mate)


def attend_earlier(visible, lengths, here, k_here, k_mate, v_here, v_mate, acc, top):
    return pl.pallas_call(
        earlier_body,
        grid=(1,),
        in_specs=[SMEM, SMEM, pl.BlockSpec((2, GROUPS, Q_ROWS, HEAD_DIM), lambda i: (0, 0, 0, 0))]
        + [WHOLE] * 6,
        out_specs=WHOLE,
        out_shape=jax.ShapeDtypeStruct((2, GROUPS, Q_ROWS, HEAD_DIM), jnp.bfloat16),
        scratch_shapes=[pltpu.VMEM(s.shape, s.dtype) for s in STATE] + [QUERY_SCRATCH],
        compiler_params=BIG,
        cost_estimate=pl.CostEstimate(flops=5 * 10**9, bytes_accessed=10**7, transcendentals=10**7),
    )(visible, lengths, here, k_here, k_mate, v_here, v_mate, acc, top)


def exchange(array):
    flat = array.reshape((2 * GROUPS,) + array.shape[2:])
    flat = lax.all_to_all(flat, ("xh", "head"), 0, 0)
    return flat.reshape(array.shape)


def to_next_plane(array):
    planes = lax.axis_size("z")
    return lax.ppermute(array, "z", [(i, i + 1) for i in range(planes - 1)])


def to_other_core(array):
    return lax.ppermute(array, "core", [(0, 1), (1, 0)])


def on_device(queries, keys, values, visible, lengths):
    v_raw = to_next_plane(values)
    here = exchange(pack(pack_all, PAYLOAD, queries, keys, values))
    k_back = to_next_plane(here[:, :, Q_ROWS : Q_ROWS + KV_ROWS])
    mate = to_other_core(here)
    v_back = exchange(pack(pack_one, KV_ROWS, v_raw))
    acc, top = attend_own(visible, lengths, here, mate)
    k_mate, v_mate = to_other_core(k_back), to_other_core(v_back)
    out = attend_earlier(visible, lengths, here, k_back, k_mate, v_back, v_mate, acc, top)
    return unpack(exchange(out))


def solution(mesh):
    planes = mesh.devices.shape[0] // PLANE
    fine = Mesh(mesh.devices.reshape(planes, 2, 2, GROUPS), AXES)
    rows = P(AXES, None)
    return jax.shard_map(
        on_device,
        mesh=fine,
        in_specs=(rows, rows, rows, P(), P()),
        out_specs=rows,
        check_vma=False,
    )
```

```python
import functools
import math

import jax
import jax.numpy as jnp
from jax import lax
from jax.experimental import pallas as pl
from jax.experimental.pallas import tpu as pltpu
from jax.sharding import Mesh
from jax.sharding import PartitionSpec as P

HEAD_DIM = 128
ROWS = 128
GROUPS = 8
HALF = ROWS // 2
CHUNK = ROWS // 4
PLANE = 4
STRETCH = GROUPS * ROWS
QUERIES = STRETCH + STRETCH // 2
TILE = 512
TILES = QUERIES // TILE
OWN_TILES = STRETCH // TILE
STEP = 256
Q_ROWS = ROWS + HALF
KV_ROWS = 2 * ROWS
PAYLOAD = Q_ROWS + 2 * KV_ROWS
BACK_ROWS = KV_ROWS + ROWS
SCALE = HEAD_DIM**-0.5 * math.log2(math.e)
LOWEST = -1e30
AXES = ("z", "xh", "core", "head")
BIG, MIDDLE, SMALL = (pltpu.CompilerParams(vmem_limit_bytes=n * 2**20) for n in (62, 36, 4))
SMEM = pl.BlockSpec(memory_space=pltpu.SMEM)
WHOLE = pl.BlockSpec(memory_space=pltpu.VMEM)
ANY = pl.BlockSpec(memory_space=pl.ANY)
HBM = pl.BlockSpec(memory_space=pltpu.HBM)


def first_pack_body(q_ref, k_ref, v_ref, out_ref, mid_ref, wide, slots, in_sem, out_sem, mid_sem):
    loads = start(
        [
            pltpu.make_async_copy(ref, wide.at[n], in_sem.at[n])
            for n, ref in enumerate((k_ref, q_ref, v_ref))
        ]
    )
    loads[0].wait()
    stores = start(
        [
            pltpu.make_async_copy(wide.at[0, :, middle(g)], mid_ref.at[g], mid_sem.at[g])
            for g in range(GROUPS)
        ]
    )
    wait(loads[1:])
    for g in range(GROUPS):
        for half in range(2):
            own = slice((3 * g + 2 * half) * HEAD_DIM, (3 * g + 2 * half + 1) * HEAD_DIM)
            slots[half, g, 0:ROWS] = wide[1, :, own]
            slots[half, g, ROWS:Q_ROWS] = wide[1, half * HALF : (half + 1) * HALF, middle(g)]
            for n, at in ((0, Q_ROWS), (2, Q_ROWS + KV_ROWS)):
                slots[half, g, at : at + ROWS] = wide[n, :, own]
                slots[half, g, at + ROWS : at + KV_ROWS] = wide[n, :, middle(g)]
            stores += store_slot(slots, out_ref, out_sem, half, g)
    wait(stores)


def back_pack_body(v_ref, mid_ref, out_ref, wide, slots, in_sem, out_sem, mid_sem):
    load = start([pltpu.make_async_copy(v_ref, wide.at[0], in_sem.at[0])])
    mids = start(
        [
            pltpu.make_async_copy(
                mid_ref, slots.at[half, :, KV_ROWS:BACK_ROWS], mid_sem.at[half]
            )
            for half in range(2)
        ]
    )
    wait(load + mids)
    stores = []
    for g in range(GROUPS):
        for half in range(2):
            own = slice((3 * g + 2 * half) * HEAD_DIM, (3 * g + 2 * half + 1) * HEAD_DIM)
            slots[half, g, 0:ROWS] = wide[0, :, own]
            slots[half, g, ROWS:KV_ROWS] = wide[0, :, middle(g)]
            stores += store_slot(slots, out_ref, out_sem, half, g)
    wait(stores)


def middle(g):
    return slice((3 * g + 1) * HEAD_DIM, (3 * g + 2) * HEAD_DIM)


def store_slot(slots, out_ref, out_sem, half, g):
    copy = pltpu.make_async_copy(slots.at[half, g], out_ref.at[half, g], out_sem.at[half, g])
    return start([copy])


def pack(body, rows, also, *arrays):
    slots = jax.ShapeDtypeStruct((2, GROUPS, rows, HEAD_DIM), jnp.bfloat16)
    middles = jax.ShapeDtypeStruct((GROUPS, ROWS, HEAD_DIM), jnp.bfloat16)
    return pl.pallas_call(
        body,
        in_specs=[HBM] * len(arrays),
        out_specs=[HBM] * (1 + also),
        out_shape=[slots, middles][: 1 + also],
        scratch_shapes=[
            pltpu.VMEM((3 if also else 1, ROWS, GROUPS * 3 * HEAD_DIM), jnp.bfloat16),
            pltpu.VMEM(slots.shape, slots.dtype),
            pltpu.SemaphoreType.DMA((3,)),
            pltpu.SemaphoreType.DMA((2, GROUPS)),
            pltpu.SemaphoreType.DMA((GROUPS,)),
        ],
        compiler_params=BIG,
    )(*arrays)


def unpack_body(in_ref, out_ref, wide, sem):
    stores = []
    for n in range(ROWS // CHUNK):
        rows = slice(n * CHUNK, (n + 1) * CHUNK)
        half, first = divmod(n * CHUNK, HALF)
        for g in range(GROUPS):
            for k in range(2):
                own = slice((3 * g + 2 * k) * HEAD_DIM, (3 * g + 2 * k + 1) * HEAD_DIM)
                wide[rows, own] = in_ref[k, g, rows]
            wide[rows, middle(g)] = in_ref[half, g, ROWS + first : ROWS + first + CHUNK]
        stores += start([pltpu.make_async_copy(wide.at[rows], out_ref.at[rows], sem.at[n])])
    wait(stores)


def unpack(array):
    wide = jax.ShapeDtypeStruct((ROWS, GROUPS * 3 * HEAD_DIM), jnp.bfloat16)
    return pl.pallas_call(
        unpack_body,
        in_specs=[WHOLE],
        out_specs=ANY,
        out_shape=wide,
        scratch_shapes=[
            pltpu.VMEM(wide.shape, wide.dtype), pltpu.SemaphoreType.DMA((ROWS // CHUNK,))
        ],
        compiler_params=SMALL,
    )(array)


def fold(slot, q_own, q_shared, acc_ref, top_ref, own, shared, count, limit):
    def score(tile):
        blocks = slice(tile * TILE // ROWS, (tile + 1) * TILE // ROWS)
        queries = q_own[slot, blocks] if tile < OWN_TILES else q_shared[slot]
        return lax.dot_general(
            queries.reshape(TILE, HEAD_DIM),
            (own if tile < OWN_TILES else shared)[0],
            (((1,), (1,)), ((), ())),
            preferred_element_type=jnp.float32,
        )

    def weigh(tile, scores):
        if limit is not None:
            head, tail = scores[:, : count - STEP], scores[:, count - STEP :]
            column = lax.broadcasted_iota(jnp.int32, tail.shape, 1)
            tail = jnp.where(column < limit - (count - STEP), tail, LOWEST)
            scores = jnp.concatenate([head, tail], 1)
        old = top_ref[slot, tile * TILE : (tile + 1) * TILE]
        new = jnp.maximum(old, jnp.max(scores, axis=1, keepdims=True) * SCALE)
        weights = jnp.exp2(scores * SCALE - jnp.concatenate([new] * (count // HEAD_DIM), 1))
        return weights.astype(jnp.bfloat16), jnp.exp2(old - new), new

    def mix(tile, weights, decay, new):
        rows = slice(tile * TILE, (tile + 1) * TILE)
        values = (own if tile < OWN_TILES else shared)[1]
        wide = jnp.concatenate([values, jnp.ones_like(values)], 1)
        mixed = jnp.dot(weights, wide, preferred_element_type=jnp.float32)
        acc_ref[slot, rows] = acc_ref[slot, rows] * jnp.concatenate([decay, decay], 1) + mixed
        top_ref[slot, rows] = new

    scores = score(0)
    for tile in range(TILES):
        ahead = score(tile + 1) if tile + 1 < TILES else None
        mix(tile, *weigh(tile, scores))
        scores = ahead


def sweep(earlier, visible_ref, lengths_ref, queries, acc_ref, top_ref, places, arrived):
    z, core = lax.axis_index("z"), lax.axis_index("core")
    acc_ref[...] = jnp.zeros_like(acc_ref)
    top_ref[...] = jnp.full_like(top_ref, LOWEST)
    for other in range(2):
        arrived(other)

        def step(n, carry):
            slot, x = n // 2, n % 2
            stretch = PLANE * z + 2 * slot + core
            reach = jnp.minimum(visible_ref[stretch], stretch)
            back = earlier * PLANE + 2 * (slot - x) + other * (2 * core - 1)
            seen = jnp.logical_and(back >= 0, back <= reach)
            length = lengths_ref[jnp.maximum(stretch - back, 0)]
            for count in range(STRETCH // 2, STRETCH + 1, STEP):
                fits = length <= count
                if count > STRETCH // 2:
                    fits = jnp.logical_and(fits, length > count - STEP)

                @pl.when(jnp.logical_and(seen, fits))
                def _():
                    def part(scr, at):
                        rows = scr[other, x, 0 : count // ROWS, at : at + ROWS]
                        return rows.reshape(count, HEAD_DIM)

                    parts = [part(*place) for place in places]
                    limit = None if count == STRETCH // 2 else length
                    fold(slot, *queries, acc_ref, top_ref, parts[:2], parts[2:], count, limit)

            return carry

        lax.fori_loop(0, 4, step, 0)


def start(copies):
    for copy in copies:
        copy.start()
    return copies


def wait(copies):
    for copy in copies:
        copy.wait()


def load_queries(here_ref, q_own, q_shared, sem):
    return start(
        [
            pltpu.make_async_copy(here_ref.at[:, :, 0:ROWS], q_own, sem.at[0]),
            pltpu.make_async_copy(here_ref.at[:, :, ROWS:Q_ROWS], q_shared, sem.at[1]),
        ]
    )


def own_body(
    visible_ref, lengths_ref, here_ref, mate_ref,
    mixed_ref, level_ref, acc_ref, top_ref, q_own, q_shared, q_sem, kv_scr, kv_sem,
):
    loads = load_queries(here_ref, q_own, q_shared, q_sem)
    loads += start(
        [
            pltpu.make_async_copy(ref.at[:, :, Q_ROWS:], kv_scr.at[n], kv_sem.at[n])
            for n, ref in enumerate((here_ref, mate_ref))
        ]
    )
    sweep(
        0, visible_ref, lengths_ref, (q_own, q_shared), acc_ref, top_ref,
        [(kv_scr, at) for at in (0, KV_ROWS, ROWS, KV_ROWS + ROWS)],
        lambda other: wait(loads[3:] if other else loads[:3]),
    )
    total = acc_ref[:, :, HEAD_DIM:]
    mixed_ref[...] = acc_ref[:, :, 0:HEAD_DIM] / total
    level_ref[...] = top_ref[...] + jnp.log2(total)


def earlier_body(
    visible_ref, lengths_ref, here_ref, k_back, k_mate, v_back, v_mate, mixed_in, level_in,
    out_ref, mixed_own, level_own, acc_ref, top_ref, q_own, q_shared, q_sem, k_scr, v_scr, kv_sem,
    own_sem,
):
    loads = load_queries(here_ref, q_own, q_shared, q_sem)
    loads += start(
        [
            pltpu.make_async_copy(ref, scr.at[n], kv_sem.at[n, m])
            for n, pair in enumerate(((k_back, v_back), (k_mate, v_mate)))
            for m, (ref, scr) in enumerate(zip(pair, (k_scr, v_scr)))
        ]
    )
    state = start(
        [
            pltpu.make_async_copy(mixed_in, mixed_own, own_sem.at[0]),
            pltpu.make_async_copy(level_in, level_own, own_sem.at[1]),
        ]
    )
    sweep(
        1, visible_ref, lengths_ref, (q_own, q_shared), acc_ref, top_ref,
        [(k_scr, 0), (v_scr, 0), (v_scr, KV_ROWS), (v_scr, ROWS)],
        lambda other: wait(loads[4:] if other else loads[:4]),
    )
    wait(state)
    z, xh, core = (lax.axis_index(name) for name in ("z", "xh", "core"))

    def token(count, step, first):
        row = lax.broadcasted_iota(jnp.int32, (count, HEAD_DIM), 0)
        return (row // step) * ROWS + first + row % step

    for slot in range(2):
        length = lengths_ref[PLANE * z + 2 * slot + core]
        for rows, tokens, height, at in (
            (slice(0, STRETCH), token(STRETCH, ROWS, 0), ROWS, 0),
            (slice(STRETCH, QUERIES), token(STRETCH // 2, HALF, xh * HALF), HALF, ROWS),
        ):
            top = jnp.maximum(top_ref[slot, rows], level_own[slot, rows])
            now, before = jnp.exp2(level_own[slot, rows] - top), jnp.exp2(top_ref[slot, rows] - top)
            mixed = mixed_own[slot, rows] * now + acc_ref[slot, rows, 0:HEAD_DIM] * before
            total = now + acc_ref[slot, rows, HEAD_DIM:] * before
            mixed = jnp.where(tokens < length, mixed / total, 0.0).astype(jnp.bfloat16)
            out_ref[slot, :, at : at + height] = mixed.reshape(GROUPS, height, HEAD_DIM)


STATE = [jax.ShapeDtypeStruct((2, QUERIES, HEAD_DIM), jnp.float32)] * 2
STATE_SCRATCH = [pltpu.VMEM((2, QUERIES, width), jnp.float32) for width in (2 * HEAD_DIM, HEAD_DIM)]
LOAD_SCRATCH = [
    pltpu.VMEM((2, GROUPS, ROWS, HEAD_DIM), jnp.bfloat16),
    pltpu.VMEM((2, GROUPS, HALF, HEAD_DIM), jnp.bfloat16),
    pltpu.SemaphoreType.DMA((2,)),
]


def key_scratch(rows):
    return pltpu.VMEM((2, 2, GROUPS, rows, HEAD_DIM), jnp.bfloat16)


COST = pl.CostEstimate(flops=10**9, bytes_accessed=10**6, transcendentals=10**6)


def attend_own(visible, lengths, here, mate):
    return pl.pallas_call(
        own_body,
        in_specs=[SMEM, SMEM, ANY, ANY],
        out_specs=[WHOLE] * 2,
        out_shape=STATE,
        scratch_shapes=STATE_SCRATCH
        + LOAD_SCRATCH
        + [key_scratch(2 * KV_ROWS), pltpu.SemaphoreType.DMA((2,))],
        compiler_params=MIDDLE,
        cost_estimate=COST,
    )(visible, lengths, here, mate)


def attend_earlier(visible, lengths, here, k_back, k_mate, v_back, v_mate, mixed, level):
    return pl.pallas_call(
        earlier_body,
        in_specs=[SMEM, SMEM] + [ANY] * 7,
        out_specs=WHOLE,
        out_shape=jax.ShapeDtypeStruct((2, GROUPS, Q_ROWS, HEAD_DIM), jnp.bfloat16),
        scratch_shapes=[pltpu.VMEM(s.shape, s.dtype) for s in STATE]
        + STATE_SCRATCH
        + LOAD_SCRATCH
        + [key_scratch(ROWS), key_scratch(BACK_ROWS)]
        + [pltpu.SemaphoreType.DMA((2, 2)), pltpu.SemaphoreType.DMA((2,))],
        compiler_params=MIDDLE,
        cost_estimate=COST,
    )(visible, lengths, here, k_back, k_mate, v_back, v_mate, mixed, level)


def tie_body(*refs):
    pass


def tie(after, *arrays):
    return pl.pallas_call(
        tie_body,
        in_specs=[ANY] * (len(arrays) + 1),
        out_specs=[ANY] * len(arrays),
        out_shape=[jax.ShapeDtypeStruct(array.shape, array.dtype) for array in arrays],
        input_output_aliases={n: n for n in range(len(arrays))},
        compiler_params=SMALL,
    )(*arrays, after)


def split_body(here_ref, _, out_ref, keys_ref, scr, in_sem, out_sem):
    def load(half):
        part = here_ref.at[half, :, Q_ROWS : Q_ROWS + ROWS]
        return pltpu.make_async_copy(part, scr.at[half], in_sem.at[half])

    loads = start([load(half) for half in range(2)])
    stores = []
    for half in range(2):
        loads[half].wait()
        stores += start(
            [pltpu.make_async_copy(scr.at[half], keys_ref.at[half], out_sem.at[half])]
        )
    wait(stores)


def split_keys(here, after):
    keys = jax.ShapeDtypeStruct((2, GROUPS, ROWS, HEAD_DIM), here.dtype)
    return pl.pallas_call(
        split_body,
        in_specs=[HBM, HBM],
        out_specs=[HBM, HBM],
        out_shape=[jax.ShapeDtypeStruct(here.shape, here.dtype), keys],
        input_output_aliases={0: 0},
        scratch_shapes=[pltpu.VMEM(keys.shape, keys.dtype)] + [pltpu.SemaphoreType.DMA((2,))] * 2,
        compiler_params=BIG,
    )(here, after)


def exchange(array):
    flat = array.reshape((2 * GROUPS,) + array.shape[2:])
    flat = lax.all_to_all(flat, ("xh", "head"), 0, 0)
    return flat.reshape(array.shape)


def to_next_plane(array):
    planes = lax.axis_size("z")
    return lax.ppermute(array, "z", [(i, i + 1) for i in range(planes - 1)])


def to_other_core(array):
    return lax.ppermute(array, "core", [(0, 1), (1, 0)])


def on_device(queries, keys, values, visible, lengths):
    v_raw = to_next_plane(values)
    packed, k_middle = pack(first_pack_body, PAYLOAD, True, queries, keys, values)
    here = exchange(packed)
    (packed,) = pack(back_pack_body, BACK_ROWS, False, v_raw, to_next_plane(k_middle))
    (here,) = tie(packed, here)
    mate = to_other_core(here)
    here, k_here = split_keys(here, mate)
    k_back, v_back = to_next_plane(k_here), exchange(packed)
    mixed, level = attend_own(visible, lengths, here, mate)
    k_back, v_back = tie(mixed, k_back, v_back)
    out = attend_earlier(
        visible, lengths, here, k_back, to_other_core(k_back), v_back, to_other_core(v_back),
        mixed, level,
    )
    return unpack(exchange(out))


def solution(mesh):
    planes = mesh.devices.shape[0] // PLANE
    fine = Mesh(mesh.devices.reshape(planes, 2, 2, GROUPS), AXES)
    rows = P(AXES, None)
    return jax.shard_map(
        on_device,
        mesh=fine,
        in_specs=(rows, rows, rows, P(), P()),
        out_specs=rows,
        check_vma=False,
    )
```

```python
import functools
import math

import jax
import jax.numpy as jnp
from jax import lax
from jax.experimental import pallas as pl
from jax.experimental.pallas import tpu as pltpu
from jax.sharding import Mesh
from jax.sharding import PartitionSpec as P

HEAD_DIM = 128
ROWS = 128
GROUPS = 8
HALF = ROWS // 2
CHUNK = ROWS // 4
PARTS = 4
PLANE = 4
STRETCH = GROUPS * ROWS
QUERIES = STRETCH + STRETCH // 2
TILE = 512
STEP = 256
SIZES = (STRETCH // 2, STRETCH - STEP, STRETCH)
Q_ROWS = ROWS + HALF
KV_ROWS = 2 * ROWS
PAYLOAD = Q_ROWS + 2 * KV_ROWS
BACK_ROWS = KV_ROWS + ROWS
SCALE = HEAD_DIM**-0.5 * math.log2(math.e)
LOWEST = -1e30
AXES = ("z", "xh", "core", "head")
BIG, MIDDLE, SMALL = (pltpu.CompilerParams(vmem_limit_bytes=n * 2**20) for n in (62, 28, 4))
SMEM = pl.BlockSpec(memory_space=pltpu.SMEM)
WHOLE = pl.BlockSpec(memory_space=pltpu.VMEM)
ANY = pl.BlockSpec(memory_space=pl.ANY)
HBM = pl.BlockSpec(memory_space=pltpu.HBM)


def first_pack_body(q_ref, k_ref, v_ref, out_ref, mid_ref, wide, slots, in_sem, out_sem, mid_sem):
    width = 3 * HEAD_DIM * GROUPS // PARTS

    def load(n, part):
        ref, columns = (k_ref, q_ref, v_ref)[n], slice(part * width, (part + 1) * width)
        return pltpu.make_async_copy(ref.at[:, columns], wide.at[n, :, columns], in_sem.at[n, part])

    loads = [start([load(n, part) for n in range(3)]) for part in range(PARTS)]
    stores = []
    for g in range(GROUPS):
        if g % (GROUPS // PARTS) == 0:
            wait(loads[g // (GROUPS // PARTS)])
        stores += start([pltpu.make_async_copy(wide.at[0, :, middle(g)], mid_ref.at[g], mid_sem.at[g])])
        for half in range(2):
            own = slice((3 * g + 2 * half) * HEAD_DIM, (3 * g + 2 * half + 1) * HEAD_DIM)
            slots[half, g, 0:ROWS] = wide[1, :, own]
            slots[half, g, ROWS:Q_ROWS] = wide[1, half * HALF : (half + 1) * HALF, middle(g)]
            for n, at in ((0, Q_ROWS), (2, Q_ROWS + KV_ROWS)):
                slots[half, g, at : at + ROWS] = wide[n, :, own]
                slots[half, g, at + ROWS : at + KV_ROWS] = wide[n, :, middle(g)]
            stores += store_slot(slots, out_ref, out_sem, half, g)
    wait(stores)


def back_pack_body(v_ref, mid_ref, out_ref, wide, slots, in_sem, out_sem, mid_sem):
    load = start([pltpu.make_async_copy(v_ref, wide.at[0], in_sem.at[0, 0])])
    mids = start(
        [
            pltpu.make_async_copy(
                mid_ref, slots.at[half, :, KV_ROWS:BACK_ROWS], mid_sem.at[half]
            )
            for half in range(2)
        ]
    )
    wait(load + mids)
    stores = []
    for g in range(GROUPS):
        for half in range(2):
            own = slice((3 * g + 2 * half) * HEAD_DIM, (3 * g + 2 * half + 1) * HEAD_DIM)
            slots[half, g, 0:ROWS] = wide[0, :, own]
            slots[half, g, ROWS:KV_ROWS] = wide[0, :, middle(g)]
            stores += store_slot(slots, out_ref, out_sem, half, g)
    wait(stores)


def middle(g):
    return slice((3 * g + 1) * HEAD_DIM, (3 * g + 2) * HEAD_DIM)


def store_slot(slots, out_ref, out_sem, half, g):
    copy = pltpu.make_async_copy(slots.at[half, g], out_ref.at[half, g], out_sem.at[half, g])
    return start([copy])


def pack(body, rows, also, *arrays):
    slots = jax.ShapeDtypeStruct((2, GROUPS, rows, HEAD_DIM), jnp.bfloat16)
    middles = jax.ShapeDtypeStruct((GROUPS, ROWS, HEAD_DIM), jnp.bfloat16)
    return pl.pallas_call(
        body,
        in_specs=[HBM] * len(arrays),
        out_specs=[HBM] * (1 + also),
        out_shape=[slots, middles][: 1 + also],
        scratch_shapes=[
            pltpu.VMEM((3 if also else 1, ROWS, GROUPS * 3 * HEAD_DIM), jnp.bfloat16),
            pltpu.VMEM(slots.shape, slots.dtype),
            pltpu.SemaphoreType.DMA((3, PARTS)),
            pltpu.SemaphoreType.DMA((2, GROUPS)),
            pltpu.SemaphoreType.DMA((GROUPS,)),
        ],
        compiler_params=BIG,
    )(*arrays)


def unpack_body(in_ref, out_ref, wide, sem):
    stores = []
    for n in range(ROWS // CHUNK):
        rows = slice(n * CHUNK, (n + 1) * CHUNK)
        half, first = divmod(n * CHUNK, HALF)
        for g in range(GROUPS):
            for k in range(2):
                own = slice((3 * g + 2 * k) * HEAD_DIM, (3 * g + 2 * k + 1) * HEAD_DIM)
                wide[rows, own] = in_ref[k, g, rows]
            wide[rows, middle(g)] = in_ref[half, g, ROWS + first : ROWS + first + CHUNK]
        stores += start([pltpu.make_async_copy(wide.at[rows], out_ref.at[rows], sem.at[n])])
    wait(stores)


def unpack(array):
    wide = jax.ShapeDtypeStruct((ROWS, GROUPS * 3 * HEAD_DIM), jnp.bfloat16)
    return pl.pallas_call(
        unpack_body,
        in_specs=[WHOLE],
        out_specs=ANY,
        out_shape=wide,
        scratch_shapes=[
            pltpu.VMEM(wide.shape, wide.dtype), pltpu.SemaphoreType.DMA((ROWS // CHUNK,))
        ],
        compiler_params=SMALL,
    )(array)


def fold(slot, q_own, q_shared, acc_ref, top_ref, own, shared, asked, count, limit):
    tiles = [(at, min(TILE, asked - at)) for at in range(0, asked, TILE)]
    tiles.append((STRETCH, asked // 2))

    def score(at, height):
        if at < STRETCH:
            queries, keys = q_own[slot, at // ROWS : (at + height) // ROWS], own[0]
        else:
            queries, keys = q_shared[slot, 0 : height // HALF], shared[0]
        return lax.dot_general(
            queries.reshape(height, HEAD_DIM),
            keys,
            (((1,), (1,)), ((), ())),
            preferred_element_type=jnp.float32,
        )

    def weigh(at, height, scores):
        if limit is not None:
            head, tail = scores[:, : count - STEP], scores[:, count - STEP :]
            column = lax.broadcasted_iota(jnp.int32, tail.shape, 1)
            tail = jnp.where(column < limit - (count - STEP), tail, LOWEST)
            scores = jnp.concatenate([head, tail], 1)
        old = top_ref[slot, at : at + height]
        new = jnp.maximum(old, jnp.max(scores, axis=1, keepdims=True) * SCALE)
        weights = jnp.exp2(scores * SCALE - jnp.concatenate([new] * (count // HEAD_DIM), 1))
        return weights.astype(jnp.bfloat16), jnp.exp2(old - new), new

    def mix(at, height, weights, decay, new):
        rows = slice(at, at + height)
        values = (own if at < STRETCH else shared)[1]
        wide = jnp.concatenate([values, jnp.ones_like(values)], 1)
        mixed = jnp.dot(weights, wide, preferred_element_type=jnp.float32)
        acc_ref[slot, rows] = acc_ref[slot, rows] * jnp.concatenate([decay, decay], 1) + mixed
        top_ref[slot, rows] = new

    scores = score(*tiles[0])
    for n, tile in enumerate(tiles):
        ahead = score(*tiles[n + 1]) if n + 1 < len(tiles) else None
        mix(*tile, *weigh(*tile, scores))
        scores = ahead


def within(length, size):
    if size == SIZES[0]:
        return length <= size
    return jnp.logical_and(length <= size, length > size - STEP)


def sweep(earlier, others, visible_ref, lengths_ref, queries, acc_ref, top_ref, places, arrived):
    z, core = lax.axis_index("z"), lax.axis_index("core")
    for n, other in enumerate(others):
        arrived(n)

        def step(m, carry):
            slot, x = m // 2, m % 2
            stretch = PLANE * z + 2 * slot + core
            reach = jnp.minimum(visible_ref[stretch], stretch)
            back = earlier * PLANE + 2 * (slot - x) + other * (2 * core - 1)
            seen = jnp.logical_and(back >= 0, back <= reach)
            length = lengths_ref[jnp.maximum(stretch - back, 0)]
            for asked in SIZES[-1:]:
                for count in SIZES:
                    fits = within(length, count)

                    @pl.when(jnp.logical_and(seen, fits))
                    def _():
                        def part(scr, at):
                            rows = scr[n, x, 0 : count // ROWS, at : at + ROWS]
                            return rows.reshape(count, HEAD_DIM)

                        parts = [part(*place) for place in places]
                        limit = None if count == SIZES[0] else length
                        fold(
                            slot, *queries, acc_ref, top_ref, parts[:2], parts[2:],
                            asked, count, limit,
                        )

            return carry

        lax.fori_loop(0, 4, step, 0)


def start(copies):
    for copy in copies:
        copy.start()
    return copies


def wait(copies):
    for copy in copies:
        copy.wait()


def load_queries(here_ref, q_own, q_shared, sem):
    return start(
        [
            pltpu.make_async_copy(here_ref.at[:, :, 0:ROWS], q_own, sem.at[0]),
            pltpu.make_async_copy(here_ref.at[:, :, ROWS:Q_ROWS], q_shared, sem.at[1]),
        ]
    )


def own_body(
    visible_ref, lengths_ref, here_ref, mate_ref,
    acc_ref, top_ref, q_own, q_shared, q_sem, kv_scr, kv_sem,
):
    loads = load_queries(here_ref, q_own, q_shared, q_sem)
    loads += start(
        [
            pltpu.make_async_copy(ref.at[:, :, Q_ROWS:], kv_scr.at[n], kv_sem.at[n])
            for n, ref in enumerate((here_ref, mate_ref))
        ]
    )
    acc_ref[...] = jnp.zeros_like(acc_ref)
    top_ref[...] = jnp.full_like(top_ref, LOWEST)
    sweep(
        0, (0, 1), visible_ref, lengths_ref, (q_own, q_shared), acc_ref, top_ref,
        [(kv_scr, at) for at in (0, KV_ROWS, ROWS, KV_ROWS + ROWS)],
        lambda n: wait(loads[3:] if n else loads[:3]),
    )


def earlier_body(
    other, visible_ref, lengths_ref, here_ref, k_ref, v_ref, acc_in, top_in, acc_ref, top_ref, *rest
):
    q_own, q_shared, q_sem, k_scr, v_scr, kv_sem = rest[-6:]
    loads = load_queries(here_ref, q_own, q_shared, q_sem)
    loads += start(
        [
            pltpu.make_async_copy(ref, scr.at[0], kv_sem.at[m])
            for m, (ref, scr) in enumerate(((k_ref, k_scr), (v_ref, v_scr)))
        ]
    )
    sweep(
        1, (other,), visible_ref, lengths_ref, (q_own, q_shared), acc_ref, top_ref,
        [(k_scr, 0), (v_scr, 0), (v_scr, KV_ROWS), (v_scr, ROWS)],
        lambda n: wait(loads),
    )
    if not other:
        return
    out_ref = rest[0]
    z, xh, core = (lax.axis_index(name) for name in ("z", "xh", "core"))

    def token(count, step, first):
        row = lax.broadcasted_iota(jnp.int32, (count, HEAD_DIM), 0)
        return (row // step) * ROWS + first + row % step

    for slot in range(2):
        length = lengths_ref[PLANE * z + 2 * slot + core]
        for rows, tokens, height, at in (
            (slice(0, STRETCH), token(STRETCH, ROWS, 0), ROWS, 0),
            (slice(STRETCH, QUERIES), token(STRETCH // 2, HALF, xh * HALF), HALF, ROWS),
        ):
            mixed, total = (
                acc_ref[slot, rows, part]
                for part in (slice(0, HEAD_DIM), slice(HEAD_DIM, 2 * HEAD_DIM))
            )
            mixed = jnp.where(tokens < length, mixed / total, 0.0).astype(jnp.bfloat16)
            out_ref[slot, :, at : at + height] = mixed.reshape(GROUPS, height, HEAD_DIM)


STATE = [
    jax.ShapeDtypeStruct((2, QUERIES, width), jnp.float32) for width in (2 * HEAD_DIM, HEAD_DIM)
]
LOAD_SCRATCH = [
    pltpu.VMEM((2, GROUPS, ROWS, HEAD_DIM), jnp.bfloat16),
    pltpu.VMEM((2, GROUPS, HALF, HEAD_DIM), jnp.bfloat16),
    pltpu.SemaphoreType.DMA((2,)),
]


def key_scratch(count, rows):
    return pltpu.VMEM((count, 2, GROUPS, rows, HEAD_DIM), jnp.bfloat16)


COST = pl.CostEstimate(flops=10**9, bytes_accessed=10**6, transcendentals=10**6)


def attend_own(visible, lengths, here, mate):
    return pl.pallas_call(
        own_body,
        in_specs=[SMEM, SMEM, ANY, ANY],
        out_specs=[WHOLE] * 2,
        out_shape=STATE,
        scratch_shapes=LOAD_SCRATCH
        + [key_scratch(2, 2 * KV_ROWS), pltpu.SemaphoreType.DMA((2,))],
        compiler_params=MIDDLE,
        cost_estimate=COST,
    )(visible, lengths, here, mate)


def attend_earlier(other, visible, lengths, here, keys, values, state):
    out = jax.ShapeDtypeStruct((2, GROUPS, Q_ROWS, HEAD_DIM), jnp.bfloat16)
    return pl.pallas_call(
        functools.partial(earlier_body, other),
        in_specs=[SMEM, SMEM] + [ANY] * 3 + [WHOLE] * 2,
        out_specs=[WHOLE] * (2 + other),
        out_shape=STATE + [out] * other,
        scratch_shapes=LOAD_SCRATCH
        + [key_scratch(1, ROWS), key_scratch(1, BACK_ROWS), pltpu.SemaphoreType.DMA((2,))],
        input_output_aliases={5: 0, 6: 1},
        compiler_params=MIDDLE,
        cost_estimate=COST,
    )(visible, lengths, here, keys, values, *state)


def tie_body(*refs):
    pass


def tie(after, *arrays):
    return pl.pallas_call(
        tie_body,
        in_specs=[ANY] * (len(arrays) + 1),
        out_specs=[ANY] * len(arrays),
        out_shape=[jax.ShapeDtypeStruct(array.shape, array.dtype) for array in arrays],
        input_output_aliases={n: n for n in range(len(arrays))},
        compiler_params=SMALL,
    )(*arrays, after)


def split_body(here_ref, _, out_ref, keys_ref, scr, in_sem, out_sem):
    def load(half):
        part = here_ref.at[half, :, Q_ROWS : Q_ROWS + ROWS]
        return pltpu.make_async_copy(part, scr.at[half], in_sem.at[half])

    loads = start([load(half) for half in range(2)])
    stores = []
    for half in range(2):
        loads[half].wait()
        stores += start(
            [pltpu.make_async_copy(scr.at[half], keys_ref.at[half], out_sem.at[half])]
        )
    wait(stores)


def split_keys(here, after):
    keys = jax.ShapeDtypeStruct((2, GROUPS, ROWS, HEAD_DIM), here.dtype)
    return pl.pallas_call(
        split_body,
        in_specs=[HBM, HBM],
        out_specs=[HBM, HBM],
        out_shape=[jax.ShapeDtypeStruct(here.shape, here.dtype), keys],
        input_output_aliases={0: 0},
        scratch_shapes=[pltpu.VMEM(keys.shape, keys.dtype)] + [pltpu.SemaphoreType.DMA((2,))] * 2,
        compiler_params=BIG,
    )(here, after)


def exchange(array):
    flat = array.reshape((2 * GROUPS,) + array.shape[2:])
    flat = lax.all_to_all(flat, ("xh", "head"), 0, 0)
    return flat.reshape(array.shape)


def to_next_plane(array):
    planes = lax.axis_size("z")
    return lax.ppermute(array, "z", [(i, i + 1) for i in range(planes - 1)])


def to_other_core(array):
    return lax.ppermute(array, "core", [(0, 1), (1, 0)])


def on_device(queries, keys, values, visible, lengths):
    v_raw = to_next_plane(values)
    packed, k_middle = pack(first_pack_body, PAYLOAD, True, queries, keys, values)
    here = exchange(packed)
    (packed,) = pack(back_pack_body, BACK_ROWS, False, v_raw, to_next_plane(k_middle))
    (here,) = tie(packed, here)
    mate = to_other_core(here)
    here, k_here = split_keys(here, mate)
    k_back, v_back = to_next_plane(k_here), exchange(packed)
    state = attend_own(visible, lengths, here, mate)
    k_back, v_back = tie(state[1], k_back, v_back)
    k_mate, v_mate = to_other_core(k_back), to_other_core(v_back)
    state = attend_earlier(0, visible, lengths, here, k_back, v_back, state)
    out = attend_earlier(1, visible, lengths, here, k_mate, v_mate, state)[2]
    return unpack(exchange(out))


def solution(mesh):
    planes = mesh.devices.shape[0] // PLANE
    fine = Mesh(mesh.devices.reshape(planes, 2, 2, GROUPS), AXES)
    rows = P(AXES, None)
    return jax.shard_map(
        on_device,
        mesh=fine,
        in_specs=(rows, rows, rows, P(), P()),
        out_specs=rows,
        check_vma=False,
    )
```

```python
import functools
import math

import jax
import jax.numpy as jnp
from jax import lax
from jax.experimental import pallas as pl
from jax.experimental.pallas import tpu as pltpu
from jax.sharding import Mesh
from jax.sharding import PartitionSpec as P

HEAD_DIM = 128
ROWS = 128
GROUPS = 8
HALF = ROWS // 2
CHUNK = ROWS // 4
PARTS = 4
PLANE = 4
STRETCH = GROUPS * ROWS
QUERIES = STRETCH + STRETCH // 2
TILE = 512
STEP = 256
SIZES = (STRETCH // 2, STRETCH - STEP, STRETCH)
Q_ROWS = ROWS + HALF
KV_ROWS = 2 * ROWS
PAYLOAD = Q_ROWS + 2 * KV_ROWS
BACK_ROWS = KV_ROWS + ROWS
SCALE = HEAD_DIM**-0.5 * math.log2(math.e)
LOWEST = -1e30
AXES = ("z", "xh", "core", "head")
BIG, MIDDLE, SMALL = (pltpu.CompilerParams(vmem_limit_bytes=n * 2**20) for n in (62, 28, 4))
SMEM = pl.BlockSpec(memory_space=pltpu.SMEM)
WHOLE = pl.BlockSpec(memory_space=pltpu.VMEM)
ANY = pl.BlockSpec(memory_space=pl.ANY)
HBM = pl.BlockSpec(memory_space=pltpu.HBM)


def first_pack_body(q_ref, k_ref, v_ref, out_ref, mid_ref, wide, slots, in_sem, out_sem, mid_sem):
    width = 3 * HEAD_DIM * GROUPS // PARTS

    def load(n, part):
        ref, columns = (k_ref, q_ref, v_ref)[n], slice(part * width, (part + 1) * width)
        return pltpu.make_async_copy(ref.at[:, columns], wide.at[n, :, columns], in_sem.at[n, part])

    loads = [start([load(n, part) for n in range(3)]) for part in range(PARTS)]
    stores = []
    for g in range(GROUPS):
        if g % (GROUPS // PARTS) == 0:
            wait(loads[g // (GROUPS // PARTS)])
        stores += start([pltpu.make_async_copy(wide.at[0, :, middle(g)], mid_ref.at[g], mid_sem.at[g])])
        for half in range(2):
            own = slice((3 * g + 2 * half) * HEAD_DIM, (3 * g + 2 * half + 1) * HEAD_DIM)
            slots[half, g, 0:ROWS] = wide[1, :, own]
            slots[half, g, ROWS:Q_ROWS] = wide[1, half * HALF : (half + 1) * HALF, middle(g)]
            for n, at in ((0, Q_ROWS), (2, Q_ROWS + KV_ROWS)):
                slots[half, g, at : at + ROWS] = wide[n, :, own]
                slots[half, g, at + ROWS : at + KV_ROWS] = wide[n, :, middle(g)]
            stores += store_slot(slots, out_ref, out_sem, half, g)
    wait(stores)


def back_pack_body(v_ref, mid_ref, out_ref, wide, slots, in_sem, out_sem, mid_sem):
    load = start([pltpu.make_async_copy(v_ref, wide.at[0], in_sem.at[0, 0])])
    mids = start(
        [
            pltpu.make_async_copy(
                mid_ref, slots.at[half, :, KV_ROWS:BACK_ROWS], mid_sem.at[half]
            )
            for half in range(2)
        ]
    )
    wait(load + mids)
    stores = []
    for g in range(GROUPS):
        for half in range(2):
            own = slice((3 * g + 2 * half) * HEAD_DIM, (3 * g + 2 * half + 1) * HEAD_DIM)
            slots[half, g, 0:ROWS] = wide[0, :, own]
            slots[half, g, ROWS:KV_ROWS] = wide[0, :, middle(g)]
            stores += store_slot(slots, out_ref, out_sem, half, g)
    wait(stores)


def middle(g):
    return slice((3 * g + 1) * HEAD_DIM, (3 * g + 2) * HEAD_DIM)


def store_slot(slots, out_ref, out_sem, half, g):
    copy = pltpu.make_async_copy(slots.at[half, g], out_ref.at[half, g], out_sem.at[half, g])
    return start([copy])


def pack(body, rows, also, *arrays):
    slots = jax.ShapeDtypeStruct((2, GROUPS, rows, HEAD_DIM), jnp.bfloat16)
    middles = jax.ShapeDtypeStruct((GROUPS, ROWS, HEAD_DIM), jnp.bfloat16)
    return pl.pallas_call(
        body,
        in_specs=[HBM] * len(arrays),
        out_specs=[HBM] * (1 + also),
        out_shape=[slots, middles][: 1 + also],
        scratch_shapes=[
            pltpu.VMEM((3 if also else 1, ROWS, GROUPS * 3 * HEAD_DIM), jnp.bfloat16),
            pltpu.VMEM(slots.shape, slots.dtype),
            pltpu.SemaphoreType.DMA((3, PARTS)),
            pltpu.SemaphoreType.DMA((2, GROUPS)),
            pltpu.SemaphoreType.DMA((GROUPS,)),
        ],
        compiler_params=BIG,
    )(*arrays)


def unpack_body(in_ref, out_ref, wide, sem):
    stores = []
    for n in range(ROWS // CHUNK):
        rows = slice(n * CHUNK, (n + 1) * CHUNK)
        half, first = divmod(n * CHUNK, HALF)
        for g in range(GROUPS):
            for k in range(2):
                own = slice((3 * g + 2 * k) * HEAD_DIM, (3 * g + 2 * k + 1) * HEAD_DIM)
                wide[rows, own] = in_ref[k, g, rows]
            wide[rows, middle(g)] = in_ref[half, g, ROWS + first : ROWS + first + CHUNK]
        stores += start([pltpu.make_async_copy(wide.at[rows], out_ref.at[rows], sem.at[n])])
    wait(stores)


def unpack(array):
    wide = jax.ShapeDtypeStruct((ROWS, GROUPS * 3 * HEAD_DIM), jnp.bfloat16)
    return pl.pallas_call(
        unpack_body,
        in_specs=[WHOLE],
        out_specs=ANY,
        out_shape=wide,
        scratch_shapes=[
            pltpu.VMEM(wide.shape, wide.dtype), pltpu.SemaphoreType.DMA((ROWS // CHUNK,))
        ],
        compiler_params=SMALL,
    )(array)


def fold(slot, q_own, q_shared, acc_ref, top_ref, own, shared, count, limit):
    tiles = [(at, TILE) for at in range(0, QUERIES, TILE)]

    def score(at, height):
        if at < STRETCH:
            queries, keys = q_own[slot, at // ROWS : (at + height) // ROWS], own[0]
        else:
            queries, keys = q_shared[slot, 0 : height // HALF], shared[0]
        return lax.dot_general(
            queries.reshape(height, HEAD_DIM),
            keys,
            (((1,), (1,)), ((), ())),
            preferred_element_type=jnp.float32,
        )

    def weigh(at, height, scores):
        if limit is not None:
            head, tail = scores[:, : count - STEP], scores[:, count - STEP :]
            column = lax.broadcasted_iota(jnp.int32, tail.shape, 1)
            tail = jnp.where(column < limit - (count - STEP), tail, LOWEST)
            scores = jnp.concatenate([head, tail], 1)
        old = top_ref[slot, at : at + height]
        new = jnp.maximum(old, jnp.max(scores, axis=1, keepdims=True) * SCALE)
        weights = jnp.exp2(scores * SCALE - jnp.concatenate([new] * (count // HEAD_DIM), 1))
        return weights.astype(jnp.bfloat16), jnp.exp2(old - new), new

    def mix(at, height, weights, decay, new):
        rows = slice(at, at + height)
        values = (own if at < STRETCH else shared)[1]
        wide = jnp.concatenate([values, jnp.ones_like(values)], 1)
        mixed = jnp.dot(weights, wide, preferred_element_type=jnp.float32)
        acc_ref[slot, rows] = acc_ref[slot, rows] * jnp.concatenate([decay, decay], 1) + mixed
        top_ref[slot, rows] = new

    scores = score(*tiles[0])
    for n, tile in enumerate(tiles):
        ahead = score(*tiles[n + 1]) if n + 1 < len(tiles) else None
        mix(*tile, *weigh(*tile, scores))
        scores = ahead


def within(length, size):
    if size == SIZES[0]:
        return length <= size
    return jnp.logical_and(length <= size, length > size - STEP)


def sweep(earlier, other, visible_ref, lengths_ref, queries, acc_ref, top_ref, places):
    z, core = lax.axis_index("z"), lax.axis_index("core")

    def step(m, carry):
        slot, x = m // 2, m % 2
        stretch = PLANE * z + 2 * slot + core
        reach = jnp.minimum(visible_ref[stretch], stretch)
        back = earlier * PLANE + 2 * (slot - x) + other * (2 * core - 1)
        seen = jnp.logical_and(back >= 0, back <= reach)
        length = lengths_ref[jnp.maximum(stretch - back, 0)]
        for count in SIZES:

            @pl.when(jnp.logical_and(seen, within(length, count)))
            def _():
                def part(ref, at):
                    rows = ref[x, 0 : count // ROWS, at : at + ROWS]
                    return rows.reshape(count, HEAD_DIM)

                parts = [part(*place) for place in places]
                limit = None if count == SIZES[0] else length
                fold(slot, *queries, acc_ref, top_ref, parts[:2], parts[2:], count, limit)

        return carry

    lax.fori_loop(0, 4, step, 0)


def start(copies):
    for copy in copies:
        copy.start()
    return copies


def wait(copies):
    for copy in copies:
        copy.wait()


def load_queries(here_ref, q_own, q_shared, sem):
    return start(
        [
            pltpu.make_async_copy(here_ref.at[:, :, 0:ROWS], q_own, sem.at[0]),
            pltpu.make_async_copy(here_ref.at[:, :, ROWS:Q_ROWS], q_shared, sem.at[1]),
        ]
    )


def clear(acc_ref, top_ref):
    acc_ref[...] = jnp.zeros_like(acc_ref)
    top_ref[...] = jnp.full_like(top_ref, LOWEST)


def own_body(
    visible_ref, lengths_ref, here_ref, mate_ref,
    mixed_ref, level_ref, done_ref, acc_ref, top_ref, q_own, q_shared, q_sem, kv_scr, kv_sem,
):
    loads = load_queries(here_ref, q_own, q_shared, q_sem)
    loads += start(
        [
            pltpu.make_async_copy(ref.at[:, :, Q_ROWS:], kv_scr.at[n], kv_sem.at[n])
            for n, ref in enumerate((here_ref, mate_ref))
        ]
    )
    clear(acc_ref, top_ref)
    for other in range(2):
        wait(loads[3:] if other else loads[:3])
        sweep(
            0, other, visible_ref, lengths_ref, (q_own, q_shared), acc_ref, top_ref,
            [(kv_scr.at[other], at) for at in (0, KV_ROWS, ROWS, KV_ROWS + ROWS)],
        )
    total = acc_ref[:, :, HEAD_DIM:]
    mixed_ref[...] = acc_ref[:, :, 0:HEAD_DIM] / total
    level_ref[...] = top_ref[...] + jnp.log2(total)
    done_ref[...] = jnp.zeros_like(done_ref)


def earlier_body(
    visible_ref, lengths_ref, k_ref, v_ref, here_ref, acc_ref, top_ref, q_own, q_shared, q_sem
):
    loads = load_queries(here_ref, q_own, q_shared, q_sem)
    clear(acc_ref, top_ref)
    wait(loads)
    sweep(
        1, 0, visible_ref, lengths_ref, (q_own, q_shared), acc_ref, top_ref,
        [(k_ref, 0), (v_ref, 0), (v_ref, KV_ROWS), (v_ref, ROWS)],
    )


def last_body(
    visible_ref, lengths_ref, k_ref, v_ref, q_own, q_shared, acc_in, top_in, mixed_in, level_in,
    out_ref, acc_ref, top_ref, mixed_own, level_own, sem,
):
    loads = start(
        [
            pltpu.make_async_copy(mixed_in, mixed_own, sem.at[0]),
            pltpu.make_async_copy(level_in, level_own, sem.at[1]),
        ]
    )
    sweep(
        1, 1, visible_ref, lengths_ref, (q_own, q_shared), acc_ref, top_ref,
        [(k_ref, 0), (v_ref, 0), (v_ref, KV_ROWS), (v_ref, ROWS)],
    )
    wait(loads)
    z, xh, core = (lax.axis_index(name) for name in ("z", "xh", "core"))

    def token(count, step, first):
        row = lax.broadcasted_iota(jnp.int32, (count, HEAD_DIM), 0)
        return (row // step) * ROWS + first + row % step

    for slot in range(2):
        length = lengths_ref[PLANE * z + 2 * slot + core]
        for rows, tokens, height, at in (
            (slice(0, STRETCH), token(STRETCH, ROWS, 0), ROWS, 0),
            (slice(STRETCH, QUERIES), token(STRETCH // 2, HALF, xh * HALF), HALF, ROWS),
        ):
            top = jnp.maximum(top_ref[slot, rows], level_own[slot, rows])
            now, before = jnp.exp2(level_own[slot, rows] - top), jnp.exp2(top_ref[slot, rows] - top)
            mixed = mixed_own[slot, rows] * now + acc_ref[slot, rows, 0:HEAD_DIM] * before
            total = now + acc_ref[slot, rows, HEAD_DIM:] * before
            mixed = jnp.where(tokens < length, mixed / total, 0.0).astype(jnp.bfloat16)
            out_ref[slot, :, at : at + height] = mixed.reshape(GROUPS, height, HEAD_DIM)


STATE = [
    jax.ShapeDtypeStruct((2, QUERIES, width), jnp.float32) for width in (2 * HEAD_DIM, HEAD_DIM)
]
QUERIES_APART = [
    jax.ShapeDtypeStruct((2, GROUPS, rows, HEAD_DIM), jnp.bfloat16) for rows in (ROWS, HALF)
]
COST = pl.CostEstimate(flops=10**9, bytes_accessed=10**6, transcendentals=10**6)


def attend_own(visible, lengths, here, mate):
    return pl.pallas_call(
        own_body,
        in_specs=[SMEM, SMEM, ANY, ANY],
        out_specs=[WHOLE] * 3,
        out_shape=[STATE[1]] * 2 + [jax.ShapeDtypeStruct((8, HEAD_DIM), jnp.float32)],
        scratch_shapes=[pltpu.VMEM(s.shape, s.dtype) for s in STATE + QUERIES_APART]
        + [
            pltpu.SemaphoreType.DMA((2,)),
            pltpu.VMEM((2, 2, GROUPS, 2 * KV_ROWS, HEAD_DIM), jnp.bfloat16),
            pltpu.SemaphoreType.DMA((2,)),
        ],
        compiler_params=MIDDLE,
        cost_estimate=COST,
    )(visible, lengths, here, mate)


def attend_earlier(visible, lengths, keys, values, here):
    return pl.pallas_call(
        earlier_body,
        in_specs=[SMEM, SMEM, WHOLE, WHOLE, HBM],
        out_specs=[WHOLE] * 4,
        out_shape=STATE + QUERIES_APART,
        scratch_shapes=[pltpu.SemaphoreType.DMA((2,))],
        compiler_params=MIDDLE,
        cost_estimate=COST,
    )(visible, lengths, keys, values, here)


def attend_last(visible, lengths, keys, values, q_own, q_shared, state, own):
    out = jax.ShapeDtypeStruct((2, GROUPS, Q_ROWS, HEAD_DIM), jnp.bfloat16)
    return pl.pallas_call(
        last_body,
        in_specs=[SMEM, SMEM] + [WHOLE] * 6 + [HBM] * 2,
        out_specs=[WHOLE] * 3,
        out_shape=[out] + STATE,
        scratch_shapes=[pltpu.VMEM(STATE[1].shape, jnp.float32)] * 2
        + [pltpu.SemaphoreType.DMA((2,))],
        input_output_aliases={6: 1, 7: 2},
        compiler_params=MIDDLE,
        cost_estimate=COST,
    )(visible, lengths, keys, values, q_own, q_shared, *state, *own)[0]


def tie_body(*refs):
    pass


def tie(after, *arrays):
    return pl.pallas_call(
        tie_body,
        in_specs=[ANY] * (len(arrays) + 1),
        out_specs=[ANY] * len(arrays),
        out_shape=[jax.ShapeDtypeStruct(array.shape, array.dtype) for array in arrays],
        input_output_aliases={n: n for n in range(len(arrays))},
        compiler_params=SMALL,
    )(*arrays, after)


def split_body(here_ref, _, out_ref, keys_ref, scr, in_sem, out_sem):
    def load(half):
        part = here_ref.at[half, :, Q_ROWS : Q_ROWS + ROWS]
        return pltpu.make_async_copy(part, scr.at[half], in_sem.at[half])

    loads = start([load(half) for half in range(2)])
    stores = []
    for half in range(2):
        loads[half].wait()
        stores += start(
            [pltpu.make_async_copy(scr.at[half], keys_ref.at[half], out_sem.at[half])]
        )
    wait(stores)


def split_keys(here, after):
    keys = jax.ShapeDtypeStruct((2, GROUPS, ROWS, HEAD_DIM), here.dtype)
    return pl.pallas_call(
        split_body,
        in_specs=[HBM, HBM],
        out_specs=[HBM, HBM],
        out_shape=[jax.ShapeDtypeStruct(here.shape, here.dtype), keys],
        input_output_aliases={0: 0},
        scratch_shapes=[pltpu.VMEM(keys.shape, keys.dtype)] + [pltpu.SemaphoreType.DMA((2,))] * 2,
        compiler_params=BIG,
    )(here, after)


def exchange(array):
    flat = array.reshape((2 * GROUPS,) + array.shape[2:])
    flat = lax.all_to_all(flat, ("xh", "head"), 0, 0)
    return flat.reshape(array.shape)


def to_next_plane(array):
    planes = lax.axis_size("z")
    return lax.ppermute(array, "z", [(i, i + 1) for i in range(planes - 1)])


def to_other_core(array):
    return lax.ppermute(array, "core", [(0, 1), (1, 0)])


def on_device(queries, keys, values, visible, lengths):
    v_raw = to_next_plane(values)
    packed, k_middle = pack(first_pack_body, PAYLOAD, True, queries, keys, values)
    here = exchange(packed)
    (packed,) = pack(back_pack_body, BACK_ROWS, False, v_raw, to_next_plane(k_middle))
    (here,) = tie(packed, here)
    mate = to_other_core(here)
    here, k_here = split_keys(here, mate)
    k_back, v_back = to_next_plane(k_here), exchange(packed)
    *own, done = attend_own(visible, lengths, here, mate)
    k_back, v_back = tie(done, k_back, v_back)
    k_mate, v_mate = to_other_core(k_back), to_other_core(v_back)
    *state, q_own, q_shared = attend_earlier(visible, lengths, k_back, v_back, here)
    out = attend_last(visible, lengths, k_mate, v_mate, q_own, q_shared, state, own)
    return unpack(exchange(out))


def solution(mesh):
    planes = mesh.devices.shape[0] // PLANE
    fine = Mesh(mesh.devices.reshape(planes, 2, 2, GROUPS), AXES)
    rows = P(AXES, None)
    return jax.shard_map(
        on_device,
        mesh=fine,
        in_specs=(rows, rows, rows, P(), P()),
        out_specs=rows,
        check_vma=False,
    )
```

```python
import functools
import math

import jax
import jax.numpy as jnp
from jax import lax
from jax.experimental import pallas as pl
from jax.experimental.pallas import tpu as pltpu
from jax.sharding import Mesh
from jax.sharding import PartitionSpec as P

HEAD_DIM = 128
ROWS = 128
GROUPS = 8
HALF = ROWS // 2
CHUNK = ROWS // 4
PARTS = 4
PLANE = 4
STRETCH = GROUPS * ROWS
QUERIES = STRETCH + STRETCH // 2
TILE = 512
STEP = 256
SIZES = (STRETCH // 2, STRETCH - STEP, STRETCH)
Q_ROWS = ROWS + HALF
KV_ROWS = 2 * ROWS
PAYLOAD = Q_ROWS + 2 * KV_ROWS
BACK_ROWS = KV_ROWS + ROWS
SCALE = HEAD_DIM**-0.5 * math.log2(math.e)
LOWEST = -1e30
AXES = ("z", "xh", "core", "head")
BIG, MIDDLE, SMALL = (pltpu.CompilerParams(vmem_limit_bytes=n * 2**20) for n in (62, 28, 4))
SMEM = pl.BlockSpec(memory_space=pltpu.SMEM)
WHOLE = pl.BlockSpec(memory_space=pltpu.VMEM)
ANY = pl.BlockSpec(memory_space=pl.ANY)
HBM = pl.BlockSpec(memory_space=pltpu.HBM)


def first_pack_body(q_ref, k_ref, v_ref, out_ref, mid_ref, wide, slots, in_sem, out_sem, mid_sem):
    width = 3 * HEAD_DIM * GROUPS // PARTS

    def load(n, part):
        ref, columns = (k_ref, q_ref, v_ref)[n], slice(part * width, (part + 1) * width)
        return pltpu.make_async_copy(ref.at[:, columns], wide.at[n, :, columns], in_sem.at[n, part])

    loads = [start([load(n, part) for n in range(3)]) for part in range(PARTS)]
    stores = []
    for g in range(GROUPS):
        if g % (GROUPS // PARTS) == 0:
            wait(loads[g // (GROUPS // PARTS)])
        stores += start([pltpu.make_async_copy(wide.at[0, :, middle(g)], mid_ref.at[g], mid_sem.at[g])])
        for half in range(2):
            own = slice((3 * g + 2 * half) * HEAD_DIM, (3 * g + 2 * half + 1) * HEAD_DIM)
            slots[half, g, 0:ROWS] = wide[1, :, own]
            slots[half, g, ROWS:Q_ROWS] = wide[1, half * HALF : (half + 1) * HALF, middle(g)]
            for n, at in ((0, Q_ROWS), (2, Q_ROWS + KV_ROWS)):
                slots[half, g, at : at + ROWS] = wide[n, :, own]
                slots[half, g, at + ROWS : at + KV_ROWS] = wide[n, :, middle(g)]
            stores += store_slot(slots, out_ref, out_sem, half, g)
    wait(stores)


def back_pack_body(v_ref, mid_ref, out_ref, wide, slots, in_sem, out_sem, mid_sem):
    load = start([pltpu.make_async_copy(v_ref, wide.at[0], in_sem.at[0, 0])])
    mids = start(
        [
            pltpu.make_async_copy(
                mid_ref, slots.at[half, :, KV_ROWS:BACK_ROWS], mid_sem.at[half]
            )
            for half in range(2)
        ]
    )
    wait(load + mids)
    stores = []
    for g in range(GROUPS):
        for half in range(2):
            own = slice((3 * g + 2 * half) * HEAD_DIM, (3 * g + 2 * half + 1) * HEAD_DIM)
            slots[half, g, 0:ROWS] = wide[0, :, own]
            slots[half, g, ROWS:KV_ROWS] = wide[0, :, middle(g)]
            stores += store_slot(slots, out_ref, out_sem, half, g)
    wait(stores)


def middle(g):
    return slice((3 * g + 1) * HEAD_DIM, (3 * g + 2) * HEAD_DIM)


def store_slot(slots, out_ref, out_sem, half, g):
    copy = pltpu.make_async_copy(slots.at[half, g], out_ref.at[half, g], out_sem.at[half, g])
    return start([copy])


def pack(body, rows, also, *arrays):
    slots = jax.ShapeDtypeStruct((2, GROUPS, rows, HEAD_DIM), jnp.bfloat16)
    middles = jax.ShapeDtypeStruct((GROUPS, ROWS, HEAD_DIM), jnp.bfloat16)
    return pl.pallas_call(
        body,
        in_specs=[HBM] * len(arrays),
        out_specs=[HBM] * (1 + also),
        out_shape=[slots, middles][: 1 + also],
        scratch_shapes=[
            pltpu.VMEM((3 if also else 1, ROWS, GROUPS * 3 * HEAD_DIM), jnp.bfloat16),
            pltpu.VMEM(slots.shape, slots.dtype),
            pltpu.SemaphoreType.DMA((3, PARTS)),
            pltpu.SemaphoreType.DMA((2, GROUPS)),
            pltpu.SemaphoreType.DMA((GROUPS,)),
        ],
        compiler_params=BIG,
    )(*arrays)


def unpack_body(in_ref, out_ref, wide, sem):
    stores = []
    for n in range(ROWS // CHUNK):
        rows = slice(n * CHUNK, (n + 1) * CHUNK)
        half, first = divmod(n * CHUNK, HALF)
        for g in range(GROUPS):
            for k in range(2):
                own = slice((3 * g + 2 * k) * HEAD_DIM, (3 * g + 2 * k + 1) * HEAD_DIM)
                wide[rows, own] = in_ref[k, g, rows]
            wide[rows, middle(g)] = in_ref[half, g, ROWS + first : ROWS + first + CHUNK]
        stores += start([pltpu.make_async_copy(wide.at[rows], out_ref.at[rows], sem.at[n])])
    wait(stores)


def unpack(array):
    wide = jax.ShapeDtypeStruct((ROWS, GROUPS * 3 * HEAD_DIM), jnp.bfloat16)
    return pl.pallas_call(
        unpack_body,
        in_specs=[WHOLE],
        out_specs=ANY,
        out_shape=wide,
        scratch_shapes=[
            pltpu.VMEM(wide.shape, wide.dtype), pltpu.SemaphoreType.DMA((ROWS // CHUNK,))
        ],
        compiler_params=SMALL,
    )(array)


def fold(slot, q_own, q_shared, acc_ref, top_ref, own, shared, asked, count, limit):
    tiles = [(at, min(TILE, asked - at)) for at in range(0, asked, TILE)]
    tiles.append((STRETCH, asked // 2))

    def score(at, height):
        if at < STRETCH:
            queries, keys = q_own[slot, at // ROWS : (at + height) // ROWS], own[0]
        else:
            queries, keys = q_shared[slot, 0 : height // HALF], shared[0]
        return lax.dot_general(
            queries.reshape(height, HEAD_DIM),
            keys,
            (((1,), (1,)), ((), ())),
            preferred_element_type=jnp.float32,
        )

    def weigh(at, height, scores):
        if limit is not None:
            head, tail = scores[:, : count - STEP], scores[:, count - STEP :]
            column = lax.broadcasted_iota(jnp.int32, tail.shape, 1)
            tail = jnp.where(column < limit - (count - STEP), tail, LOWEST)
            scores = jnp.concatenate([head, tail], 1)
        old = top_ref[slot, at : at + height]
        new = jnp.maximum(old, jnp.max(scores, axis=1, keepdims=True) * SCALE)
        weights = jnp.exp2(scores * SCALE - jnp.concatenate([new] * (count // HEAD_DIM), 1))
        return weights.astype(jnp.bfloat16), jnp.exp2(old - new), new

    def mix(at, height, weights, decay, new):
        rows = slice(at, at + height)
        values = (own if at < STRETCH else shared)[1]
        wide = jnp.concatenate([values, jnp.ones_like(values)], 1)
        mixed = jnp.dot(weights, wide, preferred_element_type=jnp.float32)
        acc_ref[slot, rows] = acc_ref[slot, rows] * jnp.concatenate([decay, decay], 1) + mixed
        top_ref[slot, rows] = new

    scores = score(*tiles[0])
    for n, tile in enumerate(tiles):
        ahead = score(*tiles[n + 1]) if n + 1 < len(tiles) else None
        mix(*tile, *weigh(*tile, scores))
        scores = ahead


def within(length, size):
    if size == SIZES[0]:
        return length <= size
    return jnp.logical_and(length <= size, length > size - STEP)


def sweep(earlier, other, visible_ref, lengths_ref, queries, acc_ref, top_ref, places):
    z, core = lax.axis_index("z"), lax.axis_index("core")

    def step(m, carry):
        slot, x = m // 2, m % 2
        stretch = PLANE * z + 2 * slot + core
        reach = jnp.minimum(visible_ref[stretch], stretch)
        back = earlier * PLANE + 2 * (slot - x) + other * (2 * core - 1)
        seen = jnp.logical_and(back >= 0, back <= reach)
        length = lengths_ref[jnp.maximum(stretch - back, 0)]
        short = lengths_ref[stretch] <= SIZES[1]
        for asked in SIZES[1 if earlier else 2 :]:
            right = seen
            if earlier:
                fewer = short if asked == SIZES[1] else jnp.logical_not(short)
                right = jnp.logical_and(seen, fewer)
            for count in SIZES:

                @pl.when(jnp.logical_and(right, within(length, count)))
                def _():
                    def part(ref, at):
                        rows = ref[x, 0 : count // ROWS, at : at + ROWS]
                        return rows.reshape(count, HEAD_DIM)

                    parts = [part(*place) for place in places]
                    limit = None if count == SIZES[0] else length
                    fold(slot, *queries, acc_ref, top_ref, parts[:2], parts[2:], asked, count, limit)

        return carry

    lax.fori_loop(0, 4, step, 0)


def start(copies):
    for copy in copies:
        copy.start()
    return copies


def wait(copies):
    for copy in copies:
        copy.wait()


def load_queries(here_ref, q_own, q_shared, sem):
    return start(
        [
            pltpu.make_async_copy(here_ref.at[:, :, 0:ROWS], q_own, sem.at[0]),
            pltpu.make_async_copy(here_ref.at[:, :, ROWS:Q_ROWS], q_shared, sem.at[1]),
        ]
    )


def clear(acc_ref, top_ref):
    acc_ref[...] = jnp.zeros_like(acc_ref)
    top_ref[...] = jnp.full_like(top_ref, LOWEST)


def own_body(
    visible_ref, lengths_ref, here_ref, mate_ref,
    mixed_ref, level_ref, done_ref, acc_ref, top_ref, q_own, q_shared, q_sem, kv_scr, kv_sem,
):
    loads = load_queries(here_ref, q_own, q_shared, q_sem)
    loads += start(
        [
            pltpu.make_async_copy(ref.at[:, :, Q_ROWS:], kv_scr.at[n], kv_sem.at[n])
            for n, ref in enumerate((here_ref, mate_ref))
        ]
    )
    clear(acc_ref, top_ref)
    for other in range(2):
        wait(loads[3:] if other else loads[:3])
        sweep(
            0, other, visible_ref, lengths_ref, (q_own, q_shared), acc_ref, top_ref,
            [(kv_scr.at[other], at) for at in (0, KV_ROWS, ROWS, KV_ROWS + ROWS)],
        )
    total = acc_ref[:, :, HEAD_DIM:]
    mixed_ref[...] = acc_ref[:, :, 0:HEAD_DIM] / total
    level_ref[...] = top_ref[...] + jnp.log2(total)
    done_ref[...] = jnp.zeros_like(done_ref)


def earlier_body(
    visible_ref, lengths_ref, k_ref, v_ref, here_ref, acc_ref, top_ref, q_own, q_shared, q_sem
):
    loads = load_queries(here_ref, q_own, q_shared, q_sem)
    clear(acc_ref, top_ref)
    wait(loads)
    sweep(
        1, 0, visible_ref, lengths_ref, (q_own, q_shared), acc_ref, top_ref,
        [(k_ref, 0), (v_ref, 0), (v_ref, KV_ROWS), (v_ref, ROWS)],
    )


def last_body(
    visible_ref, lengths_ref, k_ref, v_ref, q_own, q_shared, acc_in, top_in, mixed_in, level_in,
    out_ref, acc_ref, top_ref, mixed_own, level_own, sem,
):
    loads = start(
        [
            pltpu.make_async_copy(mixed_in, mixed_own, sem.at[0]),
            pltpu.make_async_copy(level_in, level_own, sem.at[1]),
        ]
    )
    sweep(
        1, 1, visible_ref, lengths_ref, (q_own, q_shared), acc_ref, top_ref,
        [(k_ref, 0), (v_ref, 0), (v_ref, KV_ROWS), (v_ref, ROWS)],
    )
    wait(loads)
    z, xh, core = (lax.axis_index(name) for name in ("z", "xh", "core"))

    def token(count, step, first):
        row = lax.broadcasted_iota(jnp.int32, (count, HEAD_DIM), 0)
        return (row // step) * ROWS + first + row % step

    for slot in range(2):
        length = lengths_ref[PLANE * z + 2 * slot + core]
        for rows, tokens, height, at in (
            (slice(0, STRETCH), token(STRETCH, ROWS, 0), ROWS, 0),
            (slice(STRETCH, QUERIES), token(STRETCH // 2, HALF, xh * HALF), HALF, ROWS),
        ):
            top = jnp.maximum(top_ref[slot, rows], level_own[slot, rows])
            now, before = jnp.exp2(level_own[slot, rows] - top), jnp.exp2(top_ref[slot, rows] - top)
            mixed = mixed_own[slot, rows] * now + acc_ref[slot, rows, 0:HEAD_DIM] * before
            total = now + acc_ref[slot, rows, HEAD_DIM:] * before
            mixed = jnp.where(tokens < length, mixed / total, 0.0).astype(jnp.bfloat16)
            out_ref[slot, :, at : at + height] = mixed.reshape(GROUPS, height, HEAD_DIM)


STATE = [
    jax.ShapeDtypeStruct((2, QUERIES, width), jnp.float32) for width in (2 * HEAD_DIM, HEAD_DIM)
]
QUERIES_APART = [
    jax.ShapeDtypeStruct((2, GROUPS, rows, HEAD_DIM), jnp.bfloat16) for rows in (ROWS, HALF)
]
COST = pl.CostEstimate(flops=10**9, bytes_accessed=10**6, transcendentals=10**6)


def attend_own(visible, lengths, here, mate):
    return pl.pallas_call(
        own_body,
        in_specs=[SMEM, SMEM, ANY, ANY],
        out_specs=[WHOLE] * 3,
        out_shape=[STATE[1]] * 2 + [jax.ShapeDtypeStruct((8, HEAD_DIM), jnp.float32)],
        scratch_shapes=[pltpu.VMEM(s.shape, s.dtype) for s in STATE + QUERIES_APART]
        + [
            pltpu.SemaphoreType.DMA((2,)),
            pltpu.VMEM((2, 2, GROUPS, 2 * KV_ROWS, HEAD_DIM), jnp.bfloat16),
            pltpu.SemaphoreType.DMA((2,)),
        ],
        compiler_params=MIDDLE,
        cost_estimate=COST,
    )(visible, lengths, here, mate)


def attend_earlier(visible, lengths, keys, values, here):
    return pl.pallas_call(
        earlier_body,
        in_specs=[SMEM, SMEM, WHOLE, WHOLE, HBM],
        out_specs=[WHOLE] * 4,
        out_shape=STATE + QUERIES_APART,
        scratch_shapes=[pltpu.SemaphoreType.DMA((2,))],
        compiler_params=MIDDLE,
        cost_estimate=COST,
    )(visible, lengths, keys, values, here)


def attend_last(visible, lengths, keys, values, q_own, q_shared, state, own):
    out = jax.ShapeDtypeStruct((2, GROUPS, Q_ROWS, HEAD_DIM), jnp.bfloat16)
    return pl.pallas_call(
        last_body,
        in_specs=[SMEM, SMEM] + [WHOLE] * 6 + [HBM] * 2,
        out_specs=[WHOLE] * 3,
        out_shape=[out] + STATE,
        scratch_shapes=[pltpu.VMEM(STATE[1].shape, jnp.float32)] * 2
        + [pltpu.SemaphoreType.DMA((2,))],
        input_output_aliases={6: 1, 7: 2},
        compiler_params=MIDDLE,
        cost_estimate=COST,
    )(visible, lengths, keys, values, q_own, q_shared, *state, *own)[0]


def tie_body(*refs):
    pass


def tie(after, *arrays):
    return pl.pallas_call(
        tie_body,
        in_specs=[ANY] * (len(arrays) + 1),
        out_specs=[ANY] * len(arrays),
        out_shape=[jax.ShapeDtypeStruct(array.shape, array.dtype) for array in arrays],
        input_output_aliases={n: n for n in range(len(arrays))},
        compiler_params=SMALL,
    )(*arrays, after)


def split_body(here_ref, _, out_ref, keys_ref, scr, in_sem, out_sem):
    def load(half):
        part = here_ref.at[half, :, Q_ROWS : Q_ROWS + ROWS]
        return pltpu.make_async_copy(part, scr.at[half], in_sem.at[half])

    loads = start([load(half) for half in range(2)])
    stores = []
    for half in range(2):
        loads[half].wait()
        stores += start(
            [pltpu.make_async_copy(scr.at[half], keys_ref.at[half], out_sem.at[half])]
        )
    wait(stores)


def split_keys(here, after):
    keys = jax.ShapeDtypeStruct((2, GROUPS, ROWS, HEAD_DIM), here.dtype)
    return pl.pallas_call(
        split_body,
        in_specs=[HBM, HBM],
        out_specs=[HBM, HBM],
        out_shape=[jax.ShapeDtypeStruct(here.shape, here.dtype), keys],
        input_output_aliases={0: 0},
        scratch_shapes=[pltpu.VMEM(keys.shape, keys.dtype)] + [pltpu.SemaphoreType.DMA((2,))] * 2,
        compiler_params=BIG,
    )(here, after)


def exchange(array):
    flat = array.reshape((2 * GROUPS,) + array.shape[2:])
    flat = lax.all_to_all(flat, ("xh", "head"), 0, 0)
    return flat.reshape(array.shape)


def to_next_plane(array):
    planes = lax.axis_size("z")
    return lax.ppermute(array, "z", [(i, i + 1) for i in range(planes - 1)])


def to_other_core(array):
    return lax.ppermute(array, "core", [(0, 1), (1, 0)])


def on_device(queries, keys, values, visible, lengths):
    v_raw = to_next_plane(values)
    packed, k_middle = pack(first_pack_body, PAYLOAD, True, queries, keys, values)
    here = exchange(packed)
    (packed,) = pack(back_pack_body, BACK_ROWS, False, v_raw, to_next_plane(k_middle))
    (here,) = tie(packed, here)
    mate = to_other_core(here)
    here, k_here = split_keys(here, mate)
    k_back, v_back = to_next_plane(k_here), exchange(packed)
    *own, done = attend_own(visible, lengths, here, mate)
    k_back, v_back = tie(done, k_back, v_back)
    k_mate, v_mate = to_other_core(k_back), to_other_core(v_back)
    *state, q_own, q_shared = attend_earlier(visible, lengths, k_back, v_back, here)
    out = attend_last(visible, lengths, k_mate, v_mate, q_own, q_shared, state, own)
    return unpack(exchange(out))


def solution(mesh):
    planes = mesh.devices.shape[0] // PLANE
    fine = Mesh(mesh.devices.reshape(planes, 2, 2, GROUPS), AXES)
    rows = P(AXES, None)
    return jax.shard_map(
        on_device,
        mesh=fine,
        in_specs=(rows, rows, rows, P(), P()),
        out_specs=rows,
        check_vma=False,
    )
```

```python
import functools
import math

import jax
import jax.numpy as jnp
from jax import lax
from jax.experimental import pallas as pl
from jax.experimental.pallas import tpu as pltpu
from jax.sharding import Mesh
from jax.sharding import PartitionSpec as P

HEAD_DIM = 128
ROWS = 128
GROUPS = 8
HALF = ROWS // 2
CHUNK = ROWS // 4
PARTS = 8
PLANE = 4
STRETCH = GROUPS * ROWS
QUERIES = STRETCH + STRETCH // 2
TILE = 512
STEP = 256
SIZES = (STRETCH // 2, STRETCH - STEP, STRETCH)
Q_ROWS = ROWS + HALF
KV_ROWS = 2 * ROWS
PAYLOAD = Q_ROWS + 2 * KV_ROWS
BACK_ROWS = KV_ROWS + ROWS
SCALE = HEAD_DIM**-0.5 * math.log2(math.e)
LOWEST = -1e30
AXES = ("z", "xh", "core", "head")
BIG, MIDDLE, SMALL = (pltpu.CompilerParams(vmem_limit_bytes=n * 2**20) for n in (62, 28, 4))
SMEM = pl.BlockSpec(memory_space=pltpu.SMEM)
WHOLE = pl.BlockSpec(memory_space=pltpu.VMEM)
ANY = pl.BlockSpec(memory_space=pl.ANY)
HBM = pl.BlockSpec(memory_space=pltpu.HBM)


def first_pack_body(q_ref, k_ref, v_ref, out_ref, mid_ref, wide, slots, in_sem, out_sem, mid_sem):
    width = 3 * HEAD_DIM * GROUPS // PARTS

    def load(n, part):
        ref, columns = (k_ref, q_ref, v_ref)[n], slice(part * width, (part + 1) * width)
        return pltpu.make_async_copy(ref.at[:, columns], wide.at[n, :, columns], in_sem.at[n, part])

    loads = [start([load(n, part) for n in range(3)]) for part in range(PARTS)]
    stores = []
    for g in range(GROUPS):
        if g % (GROUPS // PARTS) == 0:
            wait(loads[g // (GROUPS // PARTS)])
        stores += start([pltpu.make_async_copy(wide.at[0, :, middle(g)], mid_ref.at[g], mid_sem.at[g])])
        for half in range(2):
            own = slice((3 * g + 2 * half) * HEAD_DIM, (3 * g + 2 * half + 1) * HEAD_DIM)
            slots[half, g, 0:ROWS] = wide[1, :, own]
            slots[half, g, ROWS:Q_ROWS] = wide[1, half * HALF : (half + 1) * HALF, middle(g)]
            for n, at in ((0, Q_ROWS), (2, Q_ROWS + KV_ROWS)):
                slots[half, g, at : at + ROWS] = wide[n, :, own]
                slots[half, g, at + ROWS : at + KV_ROWS] = wide[n, :, middle(g)]
            stores += store_slot(slots, out_ref, out_sem, half, g)
    wait(stores)


def back_pack_body(v_ref, mid_ref, out_ref, wide, slots, in_sem, out_sem, mid_sem):
    load = start([pltpu.make_async_copy(v_ref, wide.at[0], in_sem.at[0, 0])])
    mids = start(
        [
            pltpu.make_async_copy(
                mid_ref, slots.at[half, :, KV_ROWS:BACK_ROWS], mid_sem.at[half]
            )
            for half in range(2)
        ]
    )
    wait(load + mids)
    stores = []
    for g in range(GROUPS):
        for half in range(2):
            own = slice((3 * g + 2 * half) * HEAD_DIM, (3 * g + 2 * half + 1) * HEAD_DIM)
            slots[half, g, 0:ROWS] = wide[0, :, own]
            slots[half, g, ROWS:KV_ROWS] = wide[0, :, middle(g)]
            stores += store_slot(slots, out_ref, out_sem, half, g)
    wait(stores)


def middle(g):
    return slice((3 * g + 1) * HEAD_DIM, (3 * g + 2) * HEAD_DIM)


def store_slot(slots, out_ref, out_sem, half, g):
    copy = pltpu.make_async_copy(slots.at[half, g], out_ref.at[half, g], out_sem.at[half, g])
    return start([copy])


def pack(body, rows, also, *arrays):
    slots = jax.ShapeDtypeStruct((2, GROUPS, rows, HEAD_DIM), jnp.bfloat16)
    middles = jax.ShapeDtypeStruct((GROUPS, ROWS, HEAD_DIM), jnp.bfloat16)
    return pl.pallas_call(
        body,
        in_specs=[HBM] * len(arrays),
        out_specs=[HBM] * (1 + also),
        out_shape=[slots, middles][: 1 + also],
        scratch_shapes=[
            pltpu.VMEM((3 if also else 1, ROWS, GROUPS * 3 * HEAD_DIM), jnp.bfloat16),
            pltpu.VMEM(slots.shape, slots.dtype),
            pltpu.SemaphoreType.DMA((3, PARTS)),
            pltpu.SemaphoreType.DMA((2, GROUPS)),
            pltpu.SemaphoreType.DMA((GROUPS,)),
        ],
        compiler_params=BIG,
    )(*arrays)


def unpack_body(in_ref, out_ref, wide, sem):
    stores = []
    for n in range(ROWS // CHUNK):
        rows = slice(n * CHUNK, (n + 1) * CHUNK)
        half, first = divmod(n * CHUNK, HALF)
        for g in range(GROUPS):
            for k in range(2):
                own = slice((3 * g + 2 * k) * HEAD_DIM, (3 * g + 2 * k + 1) * HEAD_DIM)
                wide[rows, own] = in_ref[k, g, rows]
            wide[rows, middle(g)] = in_ref[half, g, ROWS + first : ROWS + first + CHUNK]
        stores += start([pltpu.make_async_copy(wide.at[rows], out_ref.at[rows], sem.at[n])])
    wait(stores)


def unpack(array):
    wide = jax.ShapeDtypeStruct((ROWS, GROUPS * 3 * HEAD_DIM), jnp.bfloat16)
    return pl.pallas_call(
        unpack_body,
        in_specs=[WHOLE],
        out_specs=ANY,
        out_shape=wide,
        scratch_shapes=[
            pltpu.VMEM(wide.shape, wide.dtype), pltpu.SemaphoreType.DMA((ROWS // CHUNK,))
        ],
        compiler_params=SMALL,
    )(array)


def fold(slot, q_own, q_shared, acc_ref, top_ref, own, shared, count, limit):
    tiles = [(at, TILE) for at in range(0, QUERIES, TILE)]

    def score(at, height):
        if at < STRETCH:
            queries, keys = q_own[slot, at // ROWS : (at + height) // ROWS], own[0]
        else:
            queries, keys = q_shared[slot, 0 : height // HALF], shared[0]
        return lax.dot_general(
            queries.reshape(height, HEAD_DIM),
            keys,
            (((1,), (1,)), ((), ())),
            preferred_element_type=jnp.float32,
        )

    def weigh(at, height, scores):
        if limit is not None:
            head, tail = scores[:, : count - STEP], scores[:, count - STEP :]
            column = lax.broadcasted_iota(jnp.int32, tail.shape, 1)
            tail = jnp.where(column < limit - (count - STEP), tail, LOWEST)
            scores = jnp.concatenate([head, tail], 1)
        old = top_ref[slot, at : at + height]
        new = jnp.maximum(old, jnp.max(scores, axis=1, keepdims=True) * SCALE)
        weights = jnp.exp2(scores * SCALE - jnp.concatenate([new] * (count // HEAD_DIM), 1))
        return weights.astype(jnp.bfloat16), jnp.exp2(old - new), new

    def mix(at, height, weights, decay, new):
        rows = slice(at, at + height)
        values = (own if at < STRETCH else shared)[1]
        wide = jnp.concatenate([values, jnp.ones_like(values)], 1)
        mixed = jnp.dot(weights, wide, preferred_element_type=jnp.float32)
        acc_ref[slot, rows] = acc_ref[slot, rows] * jnp.concatenate([decay, decay], 1) + mixed
        top_ref[slot, rows] = new

    scores = score(*tiles[0])
    for n, tile in enumerate(tiles):
        ahead = score(*tiles[n + 1]) if n + 1 < len(tiles) else None
        mix(*tile, *weigh(*tile, scores))
        scores = ahead


def within(length, size):
    if size == SIZES[0]:
        return length <= size
    return jnp.logical_and(length <= size, length > size - STEP)


def sweep(earlier, other, visible_ref, lengths_ref, queries, acc_ref, top_ref, places):
    z, core = lax.axis_index("z"), lax.axis_index("core")

    def step(m, carry):
        slot, x = m // 2, m % 2
        stretch = PLANE * z + 2 * slot + core
        reach = jnp.minimum(visible_ref[stretch], stretch)
        back = earlier * PLANE + 2 * (slot - x) + other * (2 * core - 1)
        seen = jnp.logical_and(back >= 0, back <= reach)
        length = lengths_ref[jnp.maximum(stretch - back, 0)]
        for count in SIZES:

            @pl.when(jnp.logical_and(seen, within(length, count)))
            def _():
                def part(ref, at):
                    rows = ref[x, 0 : count // ROWS, at : at + ROWS]
                    return rows.reshape(count, HEAD_DIM)

                parts = [part(*place) for place in places]
                limit = None if count == SIZES[0] else length
                fold(slot, *queries, acc_ref, top_ref, parts[:2], parts[2:], count, limit)

        return carry

    lax.fori_loop(0, 4, step, 0)


def start(copies):
    for copy in copies:
        copy.start()
    return copies


def wait(copies):
    for copy in copies:
        copy.wait()


def load_queries(here_ref, q_own, q_shared, sem):
    return start(
        [
            pltpu.make_async_copy(here_ref.at[:, :, 0:ROWS], q_own, sem.at[0]),
            pltpu.make_async_copy(here_ref.at[:, :, ROWS:Q_ROWS], q_shared, sem.at[1]),
        ]
    )


def clear(acc_ref, top_ref):
    acc_ref[...] = jnp.zeros_like(acc_ref)
    top_ref[...] = jnp.full_like(top_ref, LOWEST)


def own_body(
    visible_ref, lengths_ref, here_ref, mate_ref,
    mixed_ref, level_ref, done_ref, acc_ref, top_ref, q_own, q_shared, q_sem, kv_scr, kv_sem,
):
    loads = load_queries(here_ref, q_own, q_shared, q_sem)
    loads += start(
        [
            pltpu.make_async_copy(ref.at[:, :, Q_ROWS:], kv_scr.at[n], kv_sem.at[n])
            for n, ref in enumerate((here_ref, mate_ref))
        ]
    )
    clear(acc_ref, top_ref)
    for other in range(2):
        wait(loads[3:] if other else loads[:3])
        sweep(
            0, other, visible_ref, lengths_ref, (q_own, q_shared), acc_ref, top_ref,
            [(kv_scr.at[other], at) for at in (0, KV_ROWS, ROWS, KV_ROWS + ROWS)],
        )
    total = acc_ref[:, :, HEAD_DIM:]
    mixed_ref[...] = acc_ref[:, :, 0:HEAD_DIM] / total
    level_ref[...] = top_ref[...] + jnp.log2(total)
    done_ref[...] = jnp.zeros_like(done_ref)


def earlier_body(
    visible_ref, lengths_ref, k_ref, v_ref, here_ref, acc_ref, top_ref, q_own, q_shared, q_sem
):
    loads = load_queries(here_ref, q_own, q_shared, q_sem)
    clear(acc_ref, top_ref)
    wait(loads)
    sweep(
        1, 0, visible_ref, lengths_ref, (q_own, q_shared), acc_ref, top_ref,
        [(k_ref, 0), (v_ref, 0), (v_ref, KV_ROWS), (v_ref, ROWS)],
    )


def last_body(
    visible_ref, lengths_ref, k_ref, v_ref, q_own, q_shared, acc_in, top_in, mixed_in, level_in,
    out_ref, acc_ref, top_ref, mixed_own, level_own, sem,
):
    loads = start(
        [
            pltpu.make_async_copy(mixed_in, mixed_own, sem.at[0]),
            pltpu.make_async_copy(level_in, level_own, sem.at[1]),
        ]
    )
    sweep(
        1, 1, visible_ref, lengths_ref, (q_own, q_shared), acc_ref, top_ref,
        [(k_ref, 0), (v_ref, 0), (v_ref, KV_ROWS), (v_ref, ROWS)],
    )
    wait(loads)
    z, xh, core = (lax.axis_index(name) for name in ("z", "xh", "core"))

    def token(count, step, first):
        row = lax.broadcasted_iota(jnp.int32, (count, HEAD_DIM), 0)
        return (row // step) * ROWS + first + row % step

    for slot in range(2):
        length = lengths_ref[PLANE * z + 2 * slot + core]
        for rows, tokens, height, at in (
            (slice(0, STRETCH), token(STRETCH, ROWS, 0), ROWS, 0),
            (slice(STRETCH, QUERIES), token(STRETCH // 2, HALF, xh * HALF), HALF, ROWS),
        ):
            top = jnp.maximum(top_ref[slot, rows], level_own[slot, rows])
            now, before = jnp.exp2(level_own[slot, rows] - top), jnp.exp2(top_ref[slot, rows] - top)
            mixed = mixed_own[slot, rows] * now + acc_ref[slot, rows, 0:HEAD_DIM] * before
            total = now + acc_ref[slot, rows, HEAD_DIM:] * before
            mixed = jnp.where(tokens < length, mixed / total, 0.0).astype(jnp.bfloat16)
            out_ref[slot, :, at : at + height] = mixed.reshape(GROUPS, height, HEAD_DIM)


STATE = [
    jax.ShapeDtypeStruct((2, QUERIES, width), jnp.float32) for width in (2 * HEAD_DIM, HEAD_DIM)
]
QUERIES_APART = [
    jax.ShapeDtypeStruct((2, GROUPS, rows, HEAD_DIM), jnp.bfloat16) for rows in (ROWS, HALF)
]
COST = pl.CostEstimate(flops=10**9, bytes_accessed=10**6, transcendentals=10**6)


def attend_own(visible, lengths, here, mate):
    return pl.pallas_call(
        own_body,
        in_specs=[SMEM, SMEM, ANY, ANY],
        out_specs=[WHOLE] * 3,
        out_shape=[STATE[1]] * 2 + [jax.ShapeDtypeStruct((8, HEAD_DIM), jnp.float32)],
        scratch_shapes=[pltpu.VMEM(s.shape, s.dtype) for s in STATE + QUERIES_APART]
        + [
            pltpu.SemaphoreType.DMA((2,)),
            pltpu.VMEM((2, 2, GROUPS, 2 * KV_ROWS, HEAD_DIM), jnp.bfloat16),
            pltpu.SemaphoreType.DMA((2,)),
        ],
        compiler_params=MIDDLE,
        cost_estimate=COST,
    )(visible, lengths, here, mate)


def attend_earlier(visible, lengths, keys, values, here):
    return pl.pallas_call(
        earlier_body,
        in_specs=[SMEM, SMEM, WHOLE, WHOLE, HBM],
        out_specs=[WHOLE] * 4,
        out_shape=STATE + QUERIES_APART,
        scratch_shapes=[pltpu.SemaphoreType.DMA((2,))],
        compiler_params=MIDDLE,
        cost_estimate=COST,
    )(visible, lengths, keys, values, here)


def attend_last(visible, lengths, keys, values, q_own, q_shared, state, own):
    out = jax.ShapeDtypeStruct((2, GROUPS, Q_ROWS, HEAD_DIM), jnp.bfloat16)
    return pl.pallas_call(
        last_body,
        in_specs=[SMEM, SMEM] + [WHOLE] * 6 + [HBM] * 2,
        out_specs=[WHOLE] * 3,
        out_shape=[out] + STATE,
        scratch_shapes=[pltpu.VMEM(STATE[1].shape, jnp.float32)] * 2
        + [pltpu.SemaphoreType.DMA((2,))],
        input_output_aliases={6: 1, 7: 2},
        compiler_params=MIDDLE,
        cost_estimate=COST,
    )(visible, lengths, keys, values, q_own, q_shared, *state, *own)[0]


def tie_body(*refs):
    pass


def tie(after, *arrays):
    return pl.pallas_call(
        tie_body,
        in_specs=[ANY] * (len(arrays) + 1),
        out_specs=[ANY] * len(arrays),
        out_shape=[jax.ShapeDtypeStruct(array.shape, array.dtype) for array in arrays],
        input_output_aliases={n: n for n in range(len(arrays))},
        compiler_params=SMALL,
    )(*arrays, after)


def split_body(here_ref, _, out_ref, keys_ref, scr, in_sem, out_sem):
    def load(half):
        part = here_ref.at[half, :, Q_ROWS : Q_ROWS + ROWS]
        return pltpu.make_async_copy(part, scr.at[half], in_sem.at[half])

    loads = start([load(half) for half in range(2)])
    stores = []
    for half in range(2):
        loads[half].wait()
        stores += start(
            [pltpu.make_async_copy(scr.at[half], keys_ref.at[half], out_sem.at[half])]
        )
    wait(stores)


def split_keys(here, after):
    keys = jax.ShapeDtypeStruct((2, GROUPS, ROWS, HEAD_DIM), here.dtype)
    return pl.pallas_call(
        split_body,
        in_specs=[HBM, HBM],
        out_specs=[HBM, HBM],
        out_shape=[jax.ShapeDtypeStruct(here.shape, here.dtype), keys],
        input_output_aliases={0: 0},
        scratch_shapes=[pltpu.VMEM(keys.shape, keys.dtype)] + [pltpu.SemaphoreType.DMA((2,))] * 2,
        compiler_params=BIG,
    )(here, after)


def exchange(array):
    flat = array.reshape((2 * GROUPS,) + array.shape[2:])
    flat = lax.all_to_all(flat, ("xh", "head"), 0, 0)
    return flat.reshape(array.shape)


def to_next_plane(array):
    planes = lax.axis_size("z")
    return lax.ppermute(array, "z", [(i, i + 1) for i in range(planes - 1)])


def to_other_core(array):
    return lax.ppermute(array, "core", [(0, 1), (1, 0)])


def on_device(queries, keys, values, visible, lengths):
    v_raw = to_next_plane(values)
    packed, k_middle = pack(first_pack_body, PAYLOAD, True, queries, keys, values)
    here = exchange(packed)
    (packed,) = pack(back_pack_body, BACK_ROWS, False, v_raw, to_next_plane(k_middle))
    (here,) = tie(packed, here)
    mate = to_other_core(here)
    here, k_here = split_keys(here, mate)
    k_back, v_back = to_next_plane(k_here), exchange(packed)
    *own, done = attend_own(visible, lengths, here, mate)
    k_back, v_back = tie(done, k_back, v_back)
    k_mate, v_mate = to_other_core(k_back), to_other_core(v_back)
    *state, q_own, q_shared = attend_earlier(visible, lengths, k_back, v_back, here)
    out = attend_last(visible, lengths, k_mate, v_mate, q_own, q_shared, state, own)
    return unpack(exchange(out))


def solution(mesh):
    planes = mesh.devices.shape[0] // PLANE
    fine = Mesh(mesh.devices.reshape(planes, 2, 2, GROUPS), AXES)
    rows = P(AXES, None)
    return jax.shard_map(
        on_device,
        mesh=fine,
        in_specs=(rows, rows, rows, P(), P()),
        out_specs=rows,
        check_vma=False,
    )
```
